32 devices in a mesh: ctx: 8 (over z, x), tp: 4 (over y, core).
Axes of the slice: x: 2, y: 2, z: 4, core: 2. Of those that a mesh axis runs over, the one named last changes fastest.
Arguments:
- queries: bfloat16 [1024, 4096], P('ctx', 'tp'), may hold values from -160 to 160
- key_rows: bfloat16 [1024, 512], P('ctx', 'tp'), may hold values from -4.5 to 4.5
- value_rows: bfloat16 [1024, 512], P('ctx', 'tp'), may hold values from -6 to 6
- doc_lengths: int32 [4], replicated, may hold values from 1 to 576, 1024 in all
- gate_input: bfloat16 [1024, 4096], P('ctx', 'tp'), may hold values from -6 to 6
- bc_input: bfloat16 [1024, 2, 2, 256], P('ctx'), may hold values from -1.796875 to 1.796875
- step_size: float32 [1024, 64], P('ctx', 'tp'), may hold values from 0.5 to 2
- decay_rate: float32 [64], P('tp'), may hold values from 0 to 1, as said below
- skip_gain: float32 [64], P('tp'), may hold values from 1 to 4
- conv_x: float32 [4, 4096], P(None, 'tp'), may hold values from -3 to 3
- conv_bc: float32 [4, 2, 2, 256], replicated, may hold values from -3 to 3
- norm_gain: float32 [4096], P('tp'), may hold values from 0.1 to 1.9
Outputs:
- mixed: bfloat16 [1024, 4096], P('ctx', 'tp')
The draws below stay inside these ranges and needn't reach their ends.
Inputs may be any that keep to these rules, and one draw needn't show every extreme that they name: `doc_lengths`: documents lie end to end in token order; the longest has exactly 576 tokens. `decay_rate`: positive rates.
All inputs are finite; a program needn't handle non-finite values.
Results may differ from the reference program's by a relative error of at most 0.02.
Values may be sent and summed in bfloat16 or wider, within the bound.
A program may use at most 128 MiB of HBM per device.

```python
import math
import jax
import jax.numpy as jnp
import numpy as np
from jax import lax

HD = 128
HQ_DEV = 8
MH_DEV = 16
P_SIZE = 64
N = 256
KW = 4
TOKENS = 1024
H = 32
KVH = 4
MH = 64
NG = 2
MOST = 576
NDOC = 4


def base_keys(key):
    return jnp.clip(jax.random.normal(key, (TOKENS, KVH * HD), jnp.float32), -4.5, 4.5)


def draw_key_rows(key, part):
    base = base_keys(key)
    return base.astype(jnp.bfloat16)


def draw_queries(key, part):
    key = jax.random.fold_in(key, 5)
    own_key = jax.random.fold_in(key, 0)
    drawn = jnp.clip(jax.random.normal(own_key, (TOKENS, H * HD), jnp.float32), -4.5, 4.5)
    return drawn.astype(jnp.bfloat16)


def draw_decay_rate(key, part):
    key = jax.random.fold_in(key, 7)
    pick_key, fast_key, slow_key = jax.random.split(key, 3)
    slow_share = 0.5
    slow_heads = jax.random.uniform(pick_key, (MH,), jnp.float32) < slow_share
    fast_rate = jnp.exp(jax.random.uniform(fast_key, (MH,), jnp.float32, math.log(1.0 / 50.0), math.log(1.0 / 30.0)))
    slow_rate = jnp.exp(jax.random.uniform(slow_key, (MH,), jnp.float32, math.log(0.05 / MOST), math.log(2.0 / MOST)))
    return jnp.where(slow_heads, slow_rate, fast_rate)


def block_levels(key, dims, pieces, smallest, high):
    loudness, own = 1.0, jax.random.fold_in(key, 6)
    for dim, blocks in pieces:
        draws = jnp.exp(jax.random.uniform(jax.random.fold_in(own, dim), (blocks,), jnp.float32, smallest / len(pieces), high / len(pieces)))
        loudness = loudness * jnp.repeat(draws, dims[dim] // blocks).reshape([-1 if axis == dim else 1 for axis in range(len(dims))])
    return loudness


def profile(amount, total, limit, slope):
    loads = [(1 << 20) // math.isqrt(rank ** slope) + 1 for rank in range(2, amount + 1)]
    spare, given = total - limit - (amount - 1), [1] * (amount - 1)
    while spare > 0:
        free = [i for i in range(amount - 1) if given[i] < limit]
        mass, left = sum([loads[i] for i in free]), spare
        for i in free:
            extra = min(limit - given[i], max(1, left * loads[i] // mass), spare)
            given[i] = given[i] + extra
            spare = spare - extra
    return np.array([limit] + given)


def ragged_sizes(rng, count, total, bound, lean):
    if count == 2:
        one = jax.random.randint(rng, (), max(1, total - bound), min(bound, total - 1) + 1)
        return jnp.stack([one, total - one])
    tallies = jnp.asarray(profile(count, total, bound, lean), jnp.int32)
    pairs = (count - 1) // 2
    giver, sink = tallies[1:1 + 2 * pairs:2], tallies[2:2 + 2 * pairs:2]
    margin = jnp.minimum(giver - 1, bound - sink)
    moved = jax.random.randint(jax.random.fold_in(rng, 1), (pairs,), 0, 1 << 20) % (margin + 1)
    tallies = tallies.at[1:1 + 2 * pairs:2].set(giver - moved).at[2:2 + 2 * pairs:2].set(sink + moved)
    return tallies[jax.random.permutation(jax.random.fold_in(rng, 2), count)]


def scatter_about(rng, shape, width, most, shards=(), kind=jnp.bfloat16):
    drawn = jax.random.normal(rng, shape, jnp.float32) * width
    if len(shards) > 0:
        drawn = block_levels(rng, shape, shards, -0.22, 0.18) * drawn
    return jnp.clip(drawn, min=-most, max=most).astype(kind)


def setup_inputs(seed: int = 0) -> dict:
    key_list = jax.random.split(jax.random.key(seed), 13)
    queries = draw_queries(jax.random.fold_in(key_list[12], 71), 0)
    key_rows = draw_key_rows(jax.random.fold_in(key_list[12], 71), 0)
    value_rows = scatter_about(key_list[2], (TOKENS, KVH * HD), 1.0, 6.0, ((0, 8), (1, 4)))
    doc_lengths = ragged_sizes(key_list[3], NDOC, TOKENS, MOST, 2).astype(jnp.int32)
    gate_input = scatter_about(key_list[4], (TOKENS, MH * P_SIZE), 1.0, 6.0, ((0, 8), (1, 4)))
    bc_input = scatter_about(key_list[5], (TOKENS, 2, NG, N), 0.3, 1.796875, ((0, 8),))
    step_size = jnp.clip(jnp.exp(math.log(2.0) - 1.3862944 * jax.random.uniform(key_list[6], (TOKENS, MH), jnp.float32) ** block_levels(key_list[6], (TOKENS, MH), ((0, 8), (1, 4)), -0.2, 0.2)), 0.5, 2.0)
    decay_rate = draw_decay_rate(jax.random.fold_in(key_list[12], 71), 0)
    skip_gain = jnp.clip(1.0 + 3.0 * jax.random.uniform(key_list[8], (MH,), jnp.float32) ** block_levels(key_list[8], (MH,), ((0, 4),), -0.2, 0.2), 1.0, 4.0)
    conv_x = scatter_about(key_list[9], (KW, MH * P_SIZE), KW ** -0.5, 3.0, ((1, 4),), jnp.float32)
    conv_bc = scatter_about(key_list[10], (KW, 2, NG, N), KW ** -0.5, 3.0, (), jnp.float32)
    norm_gain = jnp.clip(1.0 + 0.18 * jax.random.normal(key_list[11], (MH * P_SIZE,), jnp.float32), 0.1, 1.9)
    return {"queries": queries, "key_rows": key_rows, "value_rows": value_rows, "doc_lengths": doc_lengths, "gate_input": gate_input, "bc_input": bc_input, "step_size": step_size, "decay_rate": decay_rate, "skip_gain": skip_gain, "conv_x": conv_x, "conv_bc": conv_bc, "norm_gain": norm_gain}


EPSILON = 1e-05

def rounded(value):
    return lax.optimization_barrier(value.astype(jnp.bfloat16))

def start_table(doc_lengths):
    doc_ends = jnp.cumsum(doc_lengths).astype(jnp.int32)
    return doc_ends - doc_lengths

def doc_start(doc_starts, positions):
    covered = doc_starts[None, :] <= positions[:, None]
    return lax.optimization_barrier(jnp.max(jnp.where(covered, doc_starts[None, :], jnp.zeros_like(doc_starts)[None, :]), axis=1))

def attention(queries, key_rows, value_rows, doc_starts):
    query_block = math.gcd(TOKENS, 128)
    key_span = min(MOST + query_block, TOKENS)
    block_count = TOKENS // query_block
    score_scale = 1.0 / math.sqrt(HD)
    query_blocks = queries.reshape(block_count, query_block, KVH, HQ_DEV, HD)

    def visit(entries):
        block_index, block = entries
        query_start = block_index * query_block
        key_start = jnp.clip(query_start + query_block - key_span, 0, TOKENS - key_span).astype(jnp.int32)
        key_slab = lax.dynamic_slice_in_dim(key_rows, key_start, key_span, 0).reshape(key_span, KVH, HD)
        value_slab = lax.dynamic_slice_in_dim(value_rows, key_start, key_span, 0).reshape(key_span, KVH, HD)
        query_pos = (query_start + jnp.arange(query_block, dtype=jnp.int32)).astype(jnp.int32)
        key_pos = (key_start + jnp.arange(key_span, dtype=jnp.int32)).astype(jnp.int32)
        first_token = doc_start(doc_starts, query_pos)
        visible = (key_pos[None, :] <= query_pos[:, None]) & (key_pos[None, :] >= first_token[:, None])
        scores = jnp.einsum('qgjd,kgd->gjqk', block.astype(jnp.float32), key_slab.astype(jnp.float32), precision=lax.Precision.HIGHEST) * score_scale
        scores = jnp.where(visible[None, None], scores, -jnp.inf)
        maximum = lax.optimization_barrier(jnp.max(scores, axis=-1, keepdims=True))
        exponent = jnp.exp(scores - maximum)
        totals = lax.optimization_barrier(jnp.sum(exponent, axis=-1))
        weights = rounded(exponent)
        summed = jnp.einsum('gjqk,kgd->qgjd', weights.astype(jnp.float32), value_slab.astype(jnp.float32), precision=lax.Precision.HIGHEST)
        output = summed / jnp.transpose(totals, (2, 0, 1))[..., None]
        return output.reshape(query_block, KVH * HQ_DEV * HD).astype(jnp.bfloat16)
    outputs = lax.map(visit, (jnp.arange(block_count, dtype=jnp.int32), query_blocks))
    return outputs.reshape(TOKENS, H * HD)

def causal_conv(inputs, taps, first_token, positions):
    padded = jnp.concatenate([jnp.zeros((KW - 1,) + inputs.shape[1:], inputs.dtype), inputs], 0)
    accumulated = jnp.zeros(inputs.shape, jnp.float32)
    for shift_by in range(KW):
        tap_rows = padded[KW - 1 - shift_by:KW - 1 - shift_by + TOKENS].astype(jnp.float32)
        usable = (positions - shift_by >= first_token).reshape((TOKENS,) + (1,) * (inputs.ndim - 1))
        accumulated = accumulated + jnp.where(usable, tap_rows * taps[KW - 1 - shift_by], 0.0)
    return accumulated

def scan_layer(mixed_input, bc_conv, step_size, decay_rate, skip_gain, first_token):
    block_size = math.gcd(TOKENS, 256)
    block_count = TOKENS // block_size
    group_heads = 2 * MH_DEV
    input_blocks = mixed_input.reshape(block_count, block_size, MH, P_SIZE)
    bc_blocks = bc_conv.reshape(block_count, block_size, 2, NG, N)
    step_blocks = step_size.reshape(block_count, block_size, MH)
    start_blocks = first_token.reshape(block_count, block_size)
    highest = lax.Precision.HIGHEST

    def visit(state, entries):
        block_index, input_part, bc_part, step_part, start_part = entries
        block_start = block_index * block_size
        positions = (block_start + jnp.arange(block_size, dtype=jnp.int32)).astype(jnp.int32)
        log_decay = -decay_rate[None, :] * step_part
        cumulated = jnp.cumsum(log_decay, axis=0)
        b_values = bc_part[:, 0].astype(jnp.float32)
        c_values = bc_part[:, 1].astype(jnp.float32)
        gram_matrix = jnp.einsum('tgn,sgn->gts', c_values, b_values, precision=highest)
        gram_heads = jnp.repeat(gram_matrix, group_heads, axis=0)
        visible = (positions[None, :] >= start_part[:, None]) & (positions[None, :] <= positions[:, None])
        cum_heads = cumulated.T
        log_gap = jnp.where(visible[None], cum_heads[:, :, None] - cum_heads[:, None, :], -jnp.inf)
        mixing = gram_heads * jnp.exp(log_gap) * step_part.T[:, None, :]
        input_wide = input_part.astype(jnp.float32)
        inner_part = jnp.einsum('hts,shp->thp', mixing, input_wide, precision=highest)
        carry_in = (start_part < block_start).astype(jnp.float32)
        c_heads = jnp.repeat(c_values, group_heads, axis=1)
        carried_part = jnp.einsum('thn,hpn->thp', c_heads, state, precision=highest)
        carried_part = carried_part * (jnp.exp(cumulated) * carry_in[:, None])[:, :, None]
        output = inner_part + carried_part + skip_gain[None, :, None] * input_wide
        last_start = start_part[-1]
        state_weight = jnp.where((positions >= last_start)[:, None], jnp.exp(cumulated[-1][None, :] - cumulated), 0.0)
        state_weight = state_weight * step_part
        b_heads = jnp.repeat(b_values, group_heads, axis=1)
        block_state = jnp.einsum('shp,shn->hpn', state_weight[:, :, None] * input_wide, b_heads, precision=highest)
        carry_decay = jnp.where(last_start < block_start, jnp.exp(cumulated[-1]), 0.0)
        state = carry_decay[:, None, None] * state + block_state
        return (state, output)
    initial = jnp.zeros((MH, P_SIZE, N), jnp.float32)
    _, outputs = lax.scan(visit, initial, (jnp.arange(block_count, dtype=jnp.int32), input_blocks, bc_blocks, step_blocks, start_blocks))
    return outputs.reshape(TOKENS, MH * P_SIZE)

def reference(queries, key_rows, value_rows, doc_lengths, gate_input, bc_input, step_size, decay_rate, skip_gain, conv_x, conv_bc, norm_gain):
    doc_starts = start_table(doc_lengths)
    positions = jnp.arange(TOKENS, dtype=jnp.int32)
    first_token = doc_start(doc_starts, positions)
    attended = rounded(attention(queries, key_rows, value_rows, doc_starts))
    mixed_input = rounded(jax.nn.silu(causal_conv(attended, conv_x, first_token, positions)))
    bc_conv = rounded(jax.nn.silu(causal_conv(bc_input, conv_bc, first_token, positions)))
    ssm_out = scan_layer(mixed_input, bc_conv, step_size, decay_rate, skip_gain, first_token)
    gated = ssm_out * jax.nn.silu(gate_input.astype(jnp.float32))
    grouped = gated.reshape(TOKENS, NG, 2 * MH_DEV * P_SIZE)
    mean_square = lax.optimization_barrier(jnp.mean(grouped * grouped, axis=-1, keepdims=True))
    normalized = grouped * lax.rsqrt(mean_square + EPSILON)
    return (normalized.reshape(TOKENS, MH * P_SIZE) * norm_gain[None, :]).astype(jnp.bfloat16)
```

```python
import functools
import math

import jax
import jax.numpy as jnp
from jax import lax
from jax.experimental import pallas as pl
from jax.experimental.pallas import tpu as pltpu
from jax.sharding import PartitionSpec as P

EPSILON = 1e-05
NEGATIVE_FILL = -1e30


def from_behind(x, axis, by):
    size = lax.axis_size(axis)
    pairs = [(i, i + by) for i in range(size) if 0 <= i + by < size]
    return lax.ppermute(x, axis, pairs)


def prefix(x, axis, combine, identity):
    size, mine = (lax.axis_size(axis), lax.axis_index(axis))
    everything = jax.tree.map(
        lambda part, kind: lax.all_gather(part.astype(kind), axis), x, (jnp.bfloat16, jnp.bfloat16)
    )
    start = jax.tree.map(
        lambda part, zero: jnp.broadcast_to(jnp.asarray(zero, part.dtype), part.shape), x, identity
    )

    def step(k, before):
        reached = k < mine
        new = combine(
            before, jax.tree.map(lambda part, own: part[k].astype(own.dtype), everything, x)
        )
        return jax.tree.map(lambda a, b: jnp.where(reached, a, b), new, before)

    return lax.fori_loop(0, size, step, start)


def swapped(block, axis, bit):
    count = lax.axis_size(axis)
    route = []
    for low in range(count):
        high = low | 1 << bit
        if high != low and high < count:
            route += [(low, high), (high, low)]
    return lax.ppermute(block, axis, route)


def first_positions(doc_lengths, positions):
    doc_ends = jnp.cumsum(doc_lengths)
    doc_starts = doc_ends - doc_lengths
    covered = doc_starts[None, :] <= positions[:, None]
    return jnp.max(
        jnp.where(covered, doc_starts[None, :], jnp.zeros_like(doc_starts)[None, :]), axis=1
    )


def attend(
    running, key_block, value_block, key_start, query_rows, query_pos, query_first, score_scale
):
    maximum, totals, summed = running
    key_pos = key_start + jnp.arange(key_block.shape[0], dtype=jnp.int32)
    scores = (
        jnp.einsum("qhd,kd->hqk", query_rows, key_block, preferred_element_type=jnp.float32)
        * score_scale
    )
    visible = (
        (key_pos[None, :] <= query_pos[:, None]) & (key_pos[None, :] >= query_first[:, None])
    )[None]
    masked = jnp.where(visible, scores, NEGATIVE_FILL)
    new_maximum = jnp.maximum(maximum, jnp.max(masked, axis=-1))
    exponent = jnp.where(visible, jnp.exp(masked - new_maximum[..., None]), 0.0)
    factor = jnp.exp(maximum - new_maximum)
    totals = totals * factor + jnp.sum(exponent, axis=-1)
    weights = exponent.astype(jnp.bfloat16)
    summed = summed * factor[..., None] + jnp.einsum(
        "hqk,kd->hqd", weights, value_block, preferred_element_type=jnp.float32
    )
    return (new_maximum, totals, summed)


def key_folder(query_rows, query_pos, query_first, score_scale):
    query_last = jnp.max(query_pos)
    earliest = jnp.min(query_first)

    def maybe_attend(running, key_slab, value_slab, key_start):
        needed = (key_start <= query_last) & (key_start + key_slab.shape[0] > earliest)

        def compute(inner_run):
            return attend(
                inner_run,
                key_slab,
                value_slab,
                key_start,
                query_rows,
                query_pos,
                query_first,
                score_scale,
            )

        def keep(inner_run):
            return inner_run

        return lax.cond(needed, compute, keep, running)

    def fold_keys(running, pieces, offset):
        key_block, value_block = pieces
        key_count = key_block.shape[0]
        block_width = 256
        block_count = key_count // block_width

        def visit(inner_run, entries):
            block_index, key_slab, value_slab = entries
            return (maybe_attend(inner_run, key_slab, value_slab, block_index * block_width), None)

        running, _ = lax.scan(
            visit,
            running,
            (
                jnp.arange(block_count, dtype=jnp.int32),
                key_block.reshape(block_count, block_width, -1),
                value_block.reshape(block_count, block_width, -1),
            ),
        )
        return running

    return fold_keys


def finish(running, row_count):
    maximum, totals, summed = running
    output = summed / totals[..., None]
    return jnp.transpose(output, (1, 0, 2)).reshape(row_count, -1).astype(jnp.bfloat16)


def causal_local(extended, taps, positions, first_token, tap_count):
    row_count = positions.shape[0]
    accumulated = jnp.zeros((row_count,) + extended.shape[1:], jnp.float32)
    for shift_by in range(tap_count):
        tap_rows = extended[tap_count - 1 - shift_by : tap_count - 1 - shift_by + row_count].astype(
            jnp.float32
        )
        usable = (positions - shift_by >= first_token).reshape(
            (row_count,) + (1,) * (extended.ndim - 1)
        )
        accumulated = accumulated + jnp.where(
            usable, tap_rows * taps[tap_count - 1 - shift_by], 0.0
        )
    return accumulated


def combine_states(earlier, following):
    return (earlier[0] * following[0], earlier[1] * following[0][:, None, None] + following[1])


def on_device(
    queries,
    key_rows,
    value_rows,
    doc_lengths,
    gate_input,
    bc_input,
    step_size,
    decay_rate,
    skip_gain,
    conv_x,
    conv_bc,
    norm_gain,
):
    row_count = queries.shape[0]
    head_size = key_rows.shape[1]
    head_count = queries.shape[1] // head_size
    score_scale = 1.0 / math.sqrt(head_size)
    ctx_index = lax.axis_index("ctx")
    block_start = ctx_index * row_count
    own_pos = block_start + jnp.arange(row_count, dtype=jnp.int32)
    own_first = first_positions(doc_lengths, own_pos)
    initial = (
        jnp.full((head_count, row_count), NEGATIVE_FILL, jnp.float32),
        jnp.zeros((head_count, row_count), jnp.float32),
        jnp.zeros((head_count, row_count, head_size), jnp.float32),
    )
    query_rows = queries.reshape(row_count, head_count, head_size)
    running = key_folder(query_rows, own_pos, own_first, score_scale)(
        initial,
        (
            lax.all_gather(key_rows, "ctx", axis=0, tiled=True),
            lax.all_gather(value_rows, "ctx", axis=0, tiled=True),
        ),
        jnp.int32(0),
    )
    attended = finish(running, row_count)
    group_index = lax.axis_index("tp") // 2
    bc_local = lax.dynamic_index_in_dim(bc_input, group_index, 2, keepdims=False)
    conv_bc_local = lax.dynamic_index_in_dim(conv_bc, group_index, 2, keepdims=False)
    tap_count = conv_x.shape[0]
    rim_input, rim_bc = from_behind(
        (attended[row_count - tap_count + 1 :], bc_local[row_count - tap_count + 1 :]), "ctx", 1
    )
    mixed_input = jax.nn.silu(
        causal_local(
            jnp.concatenate([rim_input, attended], 0), conv_x, own_pos, own_first, tap_count
        )
    ).astype(jnp.bfloat16)
    bc_conv = jax.nn.silu(
        causal_local(
            jnp.concatenate([rim_bc, bc_local], 0), conv_bc_local, own_pos, own_first, tap_count
        )
    ).astype(jnp.bfloat16)
    heads_local = step_size.shape[1]
    input_heads = mixed_input.reshape(row_count, heads_local, -1)
    b_values = bc_conv[:, 0]
    c_values = bc_conv[:, 1]
    highest = lax.Precision.HIGHEST
    log_decay = -decay_rate[None, :] * step_size
    cumulated = jnp.cumsum(log_decay, axis=0)
    gram_matrix = jnp.dot(c_values, b_values.T, preferred_element_type=jnp.float32)
    visible = (own_pos[None, :] >= own_first[:, None]) & (own_pos[None, :] <= own_pos[:, None])
    cum_heads = cumulated.T
    log_gap = jnp.where(visible[None], cum_heads[:, :, None] - cum_heads[:, None, :], -jnp.inf)
    mixing = gram_matrix[None] * jnp.exp(log_gap) * step_size.T[:, None, :]
    input_wide = input_heads.astype(jnp.float32)
    inner_part = jnp.einsum("hts,shp->thp", mixing, input_wide, precision=highest)
    last_start = own_first[-1]
    state_weight = jnp.where(
        (own_pos >= last_start)[:, None], jnp.exp(cumulated[-1][None, :] - cumulated), 0.0
    )
    state_weight = state_weight * step_size
    block_state = jnp.einsum(
        "shp,sn->hpn",
        state_weight[:, :, None] * input_wide,
        b_values.astype(jnp.float32),
        precision=highest,
    )
    carry_decay = jnp.where(last_start < block_start, jnp.exp(cumulated[-1]), 0.0)
    identity = (jnp.ones_like(carry_decay), jnp.zeros_like(block_state))
    _, incoming = prefix((carry_decay, block_state), "ctx", combine_states, identity)
    carry_in = (own_first < block_start).astype(jnp.float32)
    carried_part = jnp.einsum(
        "tn,hpn->thp", c_values.astype(jnp.float32), incoming, precision=highest
    )
    carried_part = carried_part * (jnp.exp(cumulated) * carry_in[:, None])[:, :, None]
    ssm_out = inner_part + carried_part + skip_gain[None, :, None] * input_wide
    gated = ssm_out.reshape(row_count, -1) * jax.nn.silu(gate_input.astype(jnp.float32))
    square_sum = jnp.sum(gated * gated, axis=1)
    partner_sum = swapped(square_sum, "tp", 0)
    mean_square = (square_sum + partner_sum) / (2 * gated.shape[1])
    return (gated * lax.rsqrt(mean_square + EPSILON)[:, None] * norm_gain[None, :]).astype(
        jnp.bfloat16
    )


LANES = 128
RIM = 16
MESH = pl.DeviceIdType.MESH


def dot_nt(a, b):
    return lax.dot_general(a, b, (((1,), (1,)), ((), ())), preferred_element_type=jnp.float32)


def dot_tn(a, b):
    return lax.dot_general(a, b, (((0,), (0,)), ((), ())), preferred_element_type=jnp.float32)


def dot_nn(a, b):
    return jnp.dot(a, b, preferred_element_type=jnp.float32)


def silu(v):
    return v / (1.0 + jnp.exp(-v))


def fused_kernel(
    n,
    window,
    doc_ref,
    rate_ref,
    skip_ref,
    q_ref,
    k_ref,
    v_ref,
    gate_ref,
    bc_ref,
    dt_ref,
    taps_ref,
    bc_taps_ref,
    gain_ref,
    out_ref,
    kv,
    q_rim,
    bc_rim,
    bc_all,
    x_out,
    x_all,
    dt_all,
    y_out,
    y_all,
    gated_ref,
    sq_own,
    sq_other,
    kv_send,
    kv_recv,
    rim_send,
    rim_recv,
    bc_send,
    bc_recv,
    bc_core_send,
    bc_core_recv,
    x_send,
    x_recv,
    dt_send,
    dt_recv,
    y_send,
    y_recv,
    sq_sem,
):
    rows = q_ref.shape[0]
    me = lax.axis_index("ctx")
    tp = lax.axis_index("tp")
    core = lax.rem(tp, 2)
    group = tp // 2
    tp_other = tp + 1 - 2 * core
    parity = lax.rem(me, 2)
    pair = me + 1 - 2 * parity
    state_size = bc_all.shape[3]
    ndoc = doc_ref.shape[0]
    groups = bc_ref.shape[1] // (2 * state_size)

    def to_ctx(src, dst, send, recv, where):
        return pltpu.make_async_remote_copy(
            src_ref=src, dst_ref=dst, send_sem=send, recv_sem=recv,
            device_id=(where, tp), device_id_type=MESH)

    def to_core(src, dst, send, recv):
        return pltpu.make_async_remote_copy(
            src_ref=src, dst_ref=dst, send_sem=send, recv_sem=recv,
            device_id=(me, tp_other), device_id_type=MESH)

    barrier = pltpu.get_barrier_semaphore()
    for k in range(1, n):
        pl.semaphore_signal(
            barrier, inc=1, device_id=(lax.rem(me + k, n), tp), device_id_type=MESH)
    pl.semaphore_signal(barrier, inc=1, device_id=(me, tp_other), device_id_type=MESH)
    kv[0, 0] = k_ref[...]
    kv[0, 1] = v_ref[...]
    for r in range(1, window):
        @pl.when(me < r)
        def _():
            kv[r] = jnp.zeros(kv.shape[1:], kv.dtype)

    @pl.when(me == 0)
    def _():
        q_rim[...] = jnp.zeros(q_rim.shape, q_rim.dtype)
        bc_rim[...] = jnp.zeros(bc_rim.shape, bc_rim.dtype)

    pl.semaphore_wait(barrier, n)

    half = window // 2
    direct = []
    for k in range(1, half + 1):
        copy = to_ctx(kv.at[0], kv.at[2 * k], kv_send.at[k], kv_recv.at[2 * k],
                      jnp.minimum(me + 2 * k, n - 1))
        wanted = me + 2 * k < n
        if 2 * k >= window:
            wanted = wanted & (parity == 1)
        direct.append((wanted, copy))
    even = parity == 0
    odd = parity == 1
    relay_even = [to_ctx(kv.at[r], kv.at[r + 1], kv_send.at[half + 1 + r], kv_recv.at[r + 1], pair)
                  for r in range(0, window, 2)]
    relay_odd = [to_ctx(kv.at[r], kv.at[r - 1], kv_send.at[half + 1 + r], kv_recv.at[r - 1], pair)
                 for r in range(2, window + 1, 2)]
    nxt = jnp.minimum(me + 1, n - 1)
    rim_q = to_ctx(q_ref.at[pl.ds(rows - RIM, RIM)], q_rim, rim_send.at[0], rim_recv.at[0], nxt)
    rim_b = to_ctx(bc_ref.at[pl.ds(rows - RIM, RIM)], bc_rim, rim_send.at[1], rim_recv.at[1], nxt)

    @pl.when(me + 1 < n)
    def _():
        rim_b.start()

    @pl.when(even)
    def _():
        relay_even[0].start()

    for wanted, copy in direct:
        @pl.when(wanted)
        def _():
            copy.start()

    @pl.when(me + 1 < n)
    def _():
        rim_q.start()

    for k in range(1, n):
        d = lax.rem(me + k, n)
        to_ctx(dt_ref.at[d], dt_all.at[me], dt_send.at[k], dt_recv.at[me], d).start()
    dt_all[me] = dt_ref[me]

    starts = []
    total = jnp.int32(0)
    for i in range(ndoc):
        starts.append(total)
        total = total + doc_ref[i]

    def first_of(pos):
        first = jnp.zeros_like(pos)
        for s in starts:
            first = jnp.where(s <= pos, s, first)
        return first

    row_iota = lax.broadcasted_iota(jnp.int32, (rows, LANES), 0)
    lane_iota = lax.broadcasted_iota(jnp.int32, (rows, LANES), 1)
    base = me * rows
    own_pos = base + row_iota
    own_first = first_of(own_pos)
    tap_count = taps_ref.shape[0]
    since = own_pos - own_first

    def conv(extended, taps, wide):
        acc = None
        for m in range(tap_count):
            part = extended[8 - m: 8 - m + rows] * taps[tap_count - 1 - m: tap_count - m]
            seen = since >= m
            if wide > 1:
                seen = jnp.concatenate([seen.astype(jnp.int32)] * wide, axis=1) > 0
            part = jnp.where(seen, part, 0.0)
            acc = part if acc is None else acc + part
        return silu(acc).astype(jnp.bfloat16)

    @pl.when(me > 0)
    def _():
        rim_b.wait_recv()

    for i in range(2):
        for piece in range(state_size // LANES):
            cols = pl.ds(pl.multiple_of(
                (i * groups + group) * state_size + piece * LANES, LANES), LANES)
            extended = jnp.concatenate(
                [bc_rim[:, cols].astype(jnp.float32)[RIM - 8:], bc_ref[:, cols].astype(jnp.float32)], axis=0)
            bc_all[me, i, :, piece * LANES:(piece + 1) * LANES] = conv(extended, bc_taps_ref[:, cols], 1)

    column = [lax.rem(me + 2 * k, n) for k in range(1, n // 2)]

    def relay_bc(s, slot):
        return to_ctx(bc_all.at[s, core], bc_all.at[s, core], bc_send.at[slot], bc_recv.at[s], pair)

    def share_bc(s, slot):
        return to_core(bc_all.at[s, core], bc_all.at[s, core], bc_core_send.at[slot], bc_core_recv.at[s])

    bc_own = [to_ctx(bc_all.at[me, core], bc_all.at[me, core], bc_send.at[0], bc_recv.at[me], pair)]
    for k, d in enumerate(column):
        bc_own.append(to_ctx(bc_all.at[me, core], bc_all.at[me, core],
                             bc_send.at[1 + k], bc_recv.at[me], d))

    for r in range(2, window + 1, 2):
        cond = me >= r
        if r >= window:
            cond = cond & odd

        @pl.when(cond)
        def _():
            to_ctx(kv.at[0], kv.at[r], kv_send.at[0], kv_recv.at[r], pair).wait_recv()

        if r < window:
            @pl.when(even & (me >= r))
            def _():
                relay_even[r // 2].start()

        @pl.when(odd & (me >= r))
        def _():
            relay_odd[r // 2 - 1].start()
        if r == 2:
            for copy in bc_own:
                copy.start()
    for r in range(1, window, 2):
        @pl.when(me >= r)
        def _():
            to_ctx(kv.at[0], kv.at[r], kv_send.at[0], kv_recv.at[r], pair).wait_recv()

    @pl.when(me > 0)
    def _():
        rim_q.wait_recv()

    keys = jnp.concatenate([kv[r, 0] for r in range(window)], axis=0)
    values = jnp.concatenate([kv[r, 1] for r in range(window)], axis=0)
    scale = 1.0 / math.sqrt(k_ref.shape[1])

    def bias_of(pos):
        first = first_of(pos)
        parts = []
        for r in range(window):
            key_pos = (me - r) * rows + lane_iota
            parts.append(jnp.where((key_pos <= pos) & (key_pos >= first), 0.0, NEGATIVE_FILL))
        return jnp.concatenate(parts, axis=1)

    def attention(block, bias):
        scores = dot_nt(block, keys) * scale + bias
        exponent = jnp.exp(scores - jnp.max(scores, axis=1, keepdims=True))
        totals = jnp.sum(exponent, axis=1, keepdims=True)
        summed = dot_nn(exponent.astype(jnp.bfloat16), values)
        return (summed / totals).astype(jnp.bfloat16).astype(jnp.float32)

    rim_block = jnp.concatenate(
        [q_rim[:, h * LANES:(h + 1) * LANES] for h in range(n)], axis=0)
    rim_pos = base - RIM + lax.rem(row_iota, RIM)
    gated_ref[0] = attention(rim_block, bias_of(rim_pos))
    bias = bias_of(own_pos)

    def recv_bc(s):
        to_ctx(bc_all.at[s, core], bc_all.at[s, core], bc_send.at[0], bc_recv.at[s], pair).wait_recv()

    for k in range(n):
        h = lax.rem(me + 1 + k, n)
        cols = pl.ds(pl.multiple_of(h * LANES, LANES), LANES)
        attended = attention(q_ref[:, cols], bias)
        rim = gated_ref[0, pl.ds(pl.multiple_of(h * RIM + RIM - 8, 8), 8), :]
        x = conv(jnp.concatenate([rim, attended], axis=0), taps_ref[:, cols], 1)
        if k < n - 1:
            x_out[h] = x
            to_ctx(x_out.at[h], x_all.at[me], x_send.at[k], x_recv.at[me], h).start()
        else:
            x_all[me] = x
        if k >= n // 2 and k - n // 2 < len(column):
            s = column[k - n // 2]
            recv_bc(s)
            relay_bc(s, n // 2 + k - n // 2).start()
            share_bc(s, k - n // 2).start()
    crossed = [pair] + [lax.rem(pair + 2 * k, n) for k in range(1, n // 2)]
    for k, s in enumerate(crossed):
        recv_bc(s)
        share_bc(s, n // 2 - 1 + k).start()

    upper = (row_iota <= lane_iota).astype(jnp.float32)
    left = lane_iota < LANES // 2
    rate = [rate_ref[2 * me + a] for a in range(2)]
    skip = jnp.where(left[:1], skip_ref[2 * me], skip_ref[2 * me + 1])
    for k in range(1, n):
        s = lax.rem(me + k, n)
        to_ctx(dt_ref.at[s], dt_all.at[s], dt_send.at[k], dt_recv.at[s], s).wait_recv()
    dt_rows = [jnp.concatenate([dt_all[i, a:a + 1] for i in range(n)], axis=0) for a in range(2)]
    cum_rows = [jnp.dot(-rate[a] * dt_rows[a], upper, precision=lax.Precision.HIGHEST,
                        preferred_element_type=jnp.float32) for a in range(2)]
    state = jnp.zeros((state_size, LANES), jnp.float32)
    for i in range(n):
        @pl.when(me != i)
        def _():
            to_ctx(x_all.at[i], x_all.at[i], x_send.at[0], x_recv.at[i], pair).wait_recv()
            other = 1 - core
            to_core(bc_all.at[i, other], bc_all.at[i, other], bc_core_send.at[0],
                    bc_core_recv.at[i]).wait_recv()

        x = x_all[i]
        b, c = bc_all[i, 0], bc_all[i, 1]
        xw = x.astype(jnp.float32)
        start = i * rows
        pos = start + row_iota
        first = first_of(pos)
        key_pos = start + lane_iota
        visible = (key_pos >= first) & (key_pos <= pos)
        cum = [cum_rows[a][i:i + 1] for a in range(2)]
        dts = [dt_rows[a][i:i + 1] for a in range(2)]
        side = (rows // 2, LANES)
        cum_col = jnp.concatenate([jnp.broadcast_to(r, side) for r in cum], axis=0).T
        dt_col = jnp.concatenate([jnp.broadcast_to(r, side) for r in dts], axis=0).T
        gram = jnp.where(visible, dot_nt(c, b), 0.0)
        mix = []
        for a in range(2):
            col = cum_col[:, a * (LANES // 2):a * (LANES // 2) + 1]
            gap = jnp.where(visible, col - cum[a], 0.0)
            mix.append((gram * jnp.exp(gap) * dts[a]).astype(jnp.bfloat16))
        both = jnp.concatenate([jnp.where(left, xw, 0.0), jnp.where(left, 0.0, xw)], axis=0)
        y = dot_nn(jnp.concatenate(mix, axis=1), both.astype(jnp.bfloat16)) + skip * xw
        if i > 0:
            carried = dot_nn(c, state.astype(jnp.bfloat16))
            y = y + jnp.where(first < start, jnp.exp(cum_col), 0.0) * carried
        if i < n - 1:
            last_start = first[rows - 1:rows]
            cum_last = cum_col[rows - 1:rows]
            weight = jnp.where(pos >= last_start, jnp.exp(cum_last - cum_col) * dt_col, 0.0)
            grown = dot_tn(b, (xw * weight).astype(jnp.bfloat16))
            keep = jnp.where(last_start < start, jnp.exp(cum_last), 0.0)
            state = keep * state + grown
        y = y.astype(jnp.bfloat16)

        @pl.when(me != i)
        def _():
            y_out[i] = y
            to_ctx(y_out.at[i], y_all.at[me], y_send.at[i], y_recv.at[me], i).start()

        @pl.when(me == i)
        def _():
            y_all[me] = y

    squares = jnp.zeros((rows, LANES), jnp.float32)
    for h in range(n):
        @pl.when(me != h)
        def _():
            to_ctx(y_out.at[h], y_all.at[h], y_send.at[h], y_recv.at[h], pair).wait_recv()

        z = gate_ref[:, h * LANES:(h + 1) * LANES].astype(jnp.float32)
        gated = y_all[h].astype(jnp.float32) * silu(z)
        gated_ref[h] = gated
        squares = squares + gated * gated
    sq_own[...] = squares
    swap = to_core(sq_own, sq_other, sq_sem.at[0], sq_sem.at[1])
    swap.start()

    for wanted, copy in direct:
        @pl.when(wanted)
        def _():
            copy.wait_send()
    for j, r in enumerate(range(0, window, 2)):
        @pl.when(even & (me >= r))
        def _():
            relay_even[j].wait_send()
    for j, r in enumerate(range(2, window + 1, 2)):
        @pl.when(odd & (me >= r))
        def _():
            relay_odd[j].wait_send()

    @pl.when(me + 1 < n)
    def _():
        rim_q.wait_send()
        rim_b.wait_send()
    for copy in bc_own:
        copy.wait_send()
    for k, s in enumerate(column):
        relay_bc(s, n // 2 + k).wait_send()
        share_bc(s, k).wait_send()
    for k, s in enumerate(crossed):
        share_bc(s, n // 2 - 1 + k).wait_send()
    for k in range(n - 1):
        h = lax.rem(me + 1 + k, n)
        to_ctx(x_out.at[h], x_all.at[me], x_send.at[k], x_recv.at[me], h).wait_send()
        to_ctx(dt_ref.at[h], dt_all.at[me], dt_send.at[k + 1], dt_recv.at[me], h).wait_send()
    for i in range(n):
        @pl.when(me != i)
        def _():
            to_ctx(y_out.at[i], y_all.at[me], y_send.at[i], y_recv.at[me], i).wait_send()
    swap.wait()
    width = 2 * n * LANES
    mean_square = jnp.sum(sq_own[...] + sq_other[...], axis=1, keepdims=True) / width
    factor = lax.rsqrt(mean_square + EPSILON)
    for h in range(n):
        cols = slice(h * LANES, (h + 1) * LANES)
        out_ref[:, cols] = (gated_ref[h] * factor * gain_ref[:, cols]).astype(jnp.bfloat16)


def fused_on_device(
    queries, key_rows, value_rows, doc_lengths, gate_input, bc_input, step_size,
    decay_rate, skip_gain, conv_x, conv_bc, norm_gain,
):
    n = lax.axis_size("ctx")
    rows = queries.shape[0]
    state_size = bc_input.shape[3]
    longest = n * rows // 2 + 64
    window = 1 + -(-(longest - 1) // rows)
    bc = bc_input.reshape(rows, -1)
    dt = jnp.pad(step_size.T.reshape(n, 2, rows), ((0, 0), (0, 6), (0, 0)))
    bf16, f32 = jnp.bfloat16, jnp.float32
    vmem = pl.BlockSpec(memory_space=pltpu.VMEM)
    smem = pl.BlockSpec(memory_space=pltpu.SMEM)
    dma = pltpu.SemaphoreType.DMA
    half = window // 2
    return pl.pallas_call(
        functools.partial(fused_kernel, n, window),
        out_shape=jax.ShapeDtypeStruct(queries.shape, bf16),
        in_specs=[smem] * 3 + [vmem] * 9,
        out_specs=vmem,
        scratch_shapes=[
            pltpu.VMEM((window + 1, 2, rows, LANES), bf16),
            pltpu.VMEM((RIM, queries.shape[1]), bf16),
            pltpu.VMEM((RIM, bc.shape[1]), bf16),
            pltpu.VMEM((n, 2, rows, state_size), bf16),
            pltpu.VMEM((n, rows, LANES), bf16),
            pltpu.VMEM((n, rows, LANES), bf16),
            pltpu.VMEM((n, 8, LANES), f32),
            pltpu.VMEM((n, rows, LANES), bf16),
            pltpu.VMEM((n, rows, LANES), bf16),
            pltpu.VMEM((n, rows, LANES), f32),
            pltpu.VMEM((rows, LANES), f32),
            pltpu.VMEM((rows, LANES), f32),
            dma((half + 2 + window,)),
            dma((window + 1,)),
            dma((2,)),
            dma((2,)),
            dma((n,)),
            dma((n,)),
            dma((n,)),
            dma((n,)),
            dma((n,)),
            dma((n,)),
            dma((n,)),
            dma((n,)),
            dma((n,)),
            dma((n,)),
            dma((2,)),
        ],
        compiler_params=pltpu.CompilerParams(
            collective_id=0, has_side_effects=True, vmem_limit_bytes=32 * 1024 * 1024),
    )(
        doc_lengths, decay_rate, skip_gain, queries, key_rows, value_rows, gate_input, bc, dt,
        conv_x, conv_bc.reshape(conv_bc.shape[0], -1), norm_gain.reshape(1, -1),
    )


def plan(queries, key_rows, *rest):
    blocks = queries.shape[1] // LANES
    if blocks == lax.axis_size("ctx") and queries.shape[0] == LANES:
        return fused_on_device(queries, key_rows, *rest)
    return on_device(queries, key_rows, *rest)


def solution(mesh):
    return jax.shard_map(
        plan,
        mesh=mesh,
        in_specs=(
            P("ctx", "tp"),
            P("ctx", "tp"),
            P("ctx", "tp"),
            P(),
            P("ctx", "tp"),
            P("ctx", None, None, None),
            P("ctx", "tp"),
            P("tp"),
            P("tp"),
            P(None, "tp"),
            P(),
            P("tp"),
        ),
        out_specs=P("ctx", "tp"),
        check_vma=False,
    )
```

```python
import functools
import math

import jax
import jax.numpy as jnp
from jax import lax
from jax.experimental import pallas as pl
from jax.experimental.pallas import tpu as pltpu
from jax.sharding import PartitionSpec as P

EPSILON = 1e-05
NEGATIVE_FILL = -1e30


def from_behind(x, axis, by):
    size = lax.axis_size(axis)
    pairs = [(i, i + by) for i in range(size) if 0 <= i + by < size]
    return lax.ppermute(x, axis, pairs)


def prefix(x, axis, combine, identity):
    size, mine = (lax.axis_size(axis), lax.axis_index(axis))
    everything = jax.tree.map(
        lambda part, kind: lax.all_gather(part.astype(kind), axis), x, (jnp.bfloat16, jnp.bfloat16)
    )
    start = jax.tree.map(
        lambda part, zero: jnp.broadcast_to(jnp.asarray(zero, part.dtype), part.shape), x, identity
    )

    def step(k, before):
        reached = k < mine
        new = combine(
            before, jax.tree.map(lambda part, own: part[k].astype(own.dtype), everything, x)
        )
        return jax.tree.map(lambda a, b: jnp.where(reached, a, b), new, before)

    return lax.fori_loop(0, size, step, start)


def swapped(block, axis, bit):
    count = lax.axis_size(axis)
    route = []
    for low in range(count):
        high = low | 1 << bit
        if high != low and high < count:
            route += [(low, high), (high, low)]
    return lax.ppermute(block, axis, route)


def first_positions(doc_lengths, positions):
    doc_ends = jnp.cumsum(doc_lengths)
    doc_starts = doc_ends - doc_lengths
    covered = doc_starts[None, :] <= positions[:, None]
    return jnp.max(
        jnp.where(covered, doc_starts[None, :], jnp.zeros_like(doc_starts)[None, :]), axis=1
    )


def attend(
    running, key_block, value_block, key_start, query_rows, query_pos, query_first, score_scale
):
    maximum, totals, summed = running
    key_pos = key_start + jnp.arange(key_block.shape[0], dtype=jnp.int32)
    scores = (
        jnp.einsum("qhd,kd->hqk", query_rows, key_block, preferred_element_type=jnp.float32)
        * score_scale
    )
    visible = (
        (key_pos[None, :] <= query_pos[:, None]) & (key_pos[None, :] >= query_first[:, None])
    )[None]
    masked = jnp.where(visible, scores, NEGATIVE_FILL)
    new_maximum = jnp.maximum(maximum, jnp.max(masked, axis=-1))
    exponent = jnp.where(visible, jnp.exp(masked - new_maximum[..., None]), 0.0)
    factor = jnp.exp(maximum - new_maximum)
    totals = totals * factor + jnp.sum(exponent, axis=-1)
    weights = exponent.astype(jnp.bfloat16)
    summed = summed * factor[..., None] + jnp.einsum(
        "hqk,kd->hqd", weights, value_block, preferred_element_type=jnp.float32
    )
    return (new_maximum, totals, summed)


def key_folder(query_rows, query_pos, query_first, score_scale):
    query_last = jnp.max(query_pos)
    earliest = jnp.min(query_first)

    def maybe_attend(running, key_slab, value_slab, key_start):
        needed = (key_start <= query_last) & (key_start + key_slab.shape[0] > earliest)

        def compute(inner_run):
            return attend(
                inner_run,
                key_slab,
                value_slab,
                key_start,
                query_rows,
                query_pos,
                query_first,
                score_scale,
            )

        def keep(inner_run):
            return inner_run

        return lax.cond(needed, compute, keep, running)

    def fold_keys(running, pieces, offset):
        key_block, value_block = pieces
        key_count = key_block.shape[0]
        block_width = 256
        block_count = key_count // block_width

        def visit(inner_run, entries):
            block_index, key_slab, value_slab = entries
            return (maybe_attend(inner_run, key_slab, value_slab, block_index * block_width), None)

        running, _ = lax.scan(
            visit,
            running,
            (
                jnp.arange(block_count, dtype=jnp.int32),
                key_block.reshape(block_count, block_width, -1),
                value_block.reshape(block_count, block_width, -1),
            ),
        )
        return running

    return fold_keys


def finish(running, row_count):
    maximum, totals, summed = running
    output = summed / totals[..., None]
    return jnp.transpose(output, (1, 0, 2)).reshape(row_count, -1).astype(jnp.bfloat16)


def causal_local(extended, taps, positions, first_token, tap_count):
    row_count = positions.shape[0]
    accumulated = jnp.zeros((row_count,) + extended.shape[1:], jnp.float32)
    for shift_by in range(tap_count):
        tap_rows = extended[tap_count - 1 - shift_by : tap_count - 1 - shift_by + row_count].astype(
            jnp.float32
        )
        usable = (positions - shift_by >= first_token).reshape(
            (row_count,) + (1,) * (extended.ndim - 1)
        )
        accumulated = accumulated + jnp.where(
            usable, tap_rows * taps[tap_count - 1 - shift_by], 0.0
        )
    return accumulated


def combine_states(earlier, following):
    return (earlier[0] * following[0], earlier[1] * following[0][:, None, None] + following[1])


def on_device(
    queries,
    key_rows,
    value_rows,
    doc_lengths,
    gate_input,
    bc_input,
    step_size,
    decay_rate,
    skip_gain,
    conv_x,
    conv_bc,
    norm_gain,
):
    row_count = queries.shape[0]
    head_size = key_rows.shape[1]
    head_count = queries.shape[1] // head_size
    score_scale = 1.0 / math.sqrt(head_size)
    ctx_index = lax.axis_index("ctx")
    block_start = ctx_index * row_count
    own_pos = block_start + jnp.arange(row_count, dtype=jnp.int32)
    own_first = first_positions(doc_lengths, own_pos)
    initial = (
        jnp.full((head_count, row_count), NEGATIVE_FILL, jnp.float32),
        jnp.zeros((head_count, row_count), jnp.float32),
        jnp.zeros((head_count, row_count, head_size), jnp.float32),
    )
    query_rows = queries.reshape(row_count, head_count, head_size)
    running = key_folder(query_rows, own_pos, own_first, score_scale)(
        initial,
        (
            lax.all_gather(key_rows, "ctx", axis=0, tiled=True),
            lax.all_gather(value_rows, "ctx", axis=0, tiled=True),
        ),
        jnp.int32(0),
    )
    attended = finish(running, row_count)
    group_index = lax.axis_index("tp") // 2
    bc_local = lax.dynamic_index_in_dim(bc_input, group_index, 2, keepdims=False)
    conv_bc_local = lax.dynamic_index_in_dim(conv_bc, group_index, 2, keepdims=False)
    tap_count = conv_x.shape[0]
    rim_input, rim_bc = from_behind(
        (attended[row_count - tap_count + 1 :], bc_local[row_count - tap_count + 1 :]), "ctx", 1
    )
    mixed_input = jax.nn.silu(
        causal_local(
            jnp.concatenate([rim_input, attended], 0), conv_x, own_pos, own_first, tap_count
        )
    ).astype(jnp.bfloat16)
    bc_conv = jax.nn.silu(
        causal_local(
            jnp.concatenate([rim_bc, bc_local], 0), conv_bc_local, own_pos, own_first, tap_count
        )
    ).astype(jnp.bfloat16)
    heads_local = step_size.shape[1]
    input_heads = mixed_input.reshape(row_count, heads_local, -1)
    b_values = bc_conv[:, 0]
    c_values = bc_conv[:, 1]
    highest = lax.Precision.HIGHEST
    log_decay = -decay_rate[None, :] * step_size
    cumulated = jnp.cumsum(log_decay, axis=0)
    gram_matrix = jnp.dot(c_values, b_values.T, preferred_element_type=jnp.float32)
    visible = (own_pos[None, :] >= own_first[:, None]) & (own_pos[None, :] <= own_pos[:, None])
    cum_heads = cumulated.T
    log_gap = jnp.where(visible[None], cum_heads[:, :, None] - cum_heads[:, None, :], -jnp.inf)
    mixing = gram_matrix[None] * jnp.exp(log_gap) * step_size.T[:, None, :]
    input_wide = input_heads.astype(jnp.float32)
    inner_part = jnp.einsum("hts,shp->thp", mixing, input_wide, precision=highest)
    last_start = own_first[-1]
    state_weight = jnp.where(
        (own_pos >= last_start)[:, None], jnp.exp(cumulated[-1][None, :] - cumulated), 0.0
    )
    state_weight = state_weight * step_size
    block_state = jnp.einsum(
        "shp,sn->hpn",
        state_weight[:, :, None] * input_wide,
        b_values.astype(jnp.float32),
        precision=highest,
    )
    carry_decay = jnp.where(last_start < block_start, jnp.exp(cumulated[-1]), 0.0)
    identity = (jnp.ones_like(carry_decay), jnp.zeros_like(block_state))
    _, incoming = prefix((carry_decay, block_state), "ctx", combine_states, identity)
    carry_in = (own_first < block_start).astype(jnp.float32)
    carried_part = jnp.einsum(
        "tn,hpn->thp", c_values.astype(jnp.float32), incoming, precision=highest
    )
    carried_part = carried_part * (jnp.exp(cumulated) * carry_in[:, None])[:, :, None]
    ssm_out = inner_part + carried_part + skip_gain[None, :, None] * input_wide
    gated = ssm_out.reshape(row_count, -1) * jax.nn.silu(gate_input.astype(jnp.float32))
    square_sum = jnp.sum(gated * gated, axis=1)
    partner_sum = swapped(square_sum, "tp", 0)
    mean_square = (square_sum + partner_sum) / (2 * gated.shape[1])
    return (gated * lax.rsqrt(mean_square + EPSILON)[:, None] * norm_gain[None, :]).astype(
        jnp.bfloat16
    )


LANES = 128
RIM = 16
MESH = pl.DeviceIdType.MESH


def dot_nt(a, b):
    return lax.dot_general(a, b, (((1,), (1,)), ((), ())), preferred_element_type=jnp.float32)


def dot_tn(a, b):
    return lax.dot_general(a, b, (((0,), (0,)), ((), ())), preferred_element_type=jnp.float32)


def dot_nn(a, b):
    return jnp.dot(a, b, preferred_element_type=jnp.float32)


def silu(v):
    return v / (1.0 + jnp.exp(-v))


def fused_kernel(
    n,
    window,
    doc_ref,
    rate_ref,
    skip_ref,
    q_ref,
    k_ref,
    v_ref,
    gate_ref,
    bc_ref,
    step_ref,
    taps_ref,
    bc_taps_ref,
    gain_ref,
    out_ref,
    kv,
    q_rim,
    bc_rim,
    bc_all,
    x_out,
    x_all,
    dt_own,
    dt_all,
    mix_ref,
    weight_ref,
    carry_ref,
    state_ref,
    y_out,
    y_all,
    gated_ref,
    sq_own,
    sq_other,
    kv_send,
    kv_recv,
    rim_send,
    rim_recv,
    bc_send,
    bc_recv,
    bc_core_send,
    bc_core_recv,
    x_send,
    x_recv,
    dt_send,
    dt_recv,
    y_send,
    y_recv,
    sq_sem,
):
    rows = q_ref.shape[0]
    me = lax.axis_index("ctx")
    tp = lax.axis_index("tp")
    core = lax.rem(tp, 2)
    group = tp // 2
    tp_other = tp + 1 - 2 * core
    parity = lax.rem(me, 2)
    pair = me + 1 - 2 * parity
    state_size = bc_all.shape[3]
    ndoc = doc_ref.shape[0]
    groups = bc_ref.shape[1] // (2 * state_size)

    def to_ctx(src, dst, send, recv, where):
        return pltpu.make_async_remote_copy(
            src_ref=src, dst_ref=dst, send_sem=send, recv_sem=recv,
            device_id=(where, tp), device_id_type=MESH)

    def to_core(src, dst, send, recv):
        return pltpu.make_async_remote_copy(
            src_ref=src, dst_ref=dst, send_sem=send, recv_sem=recv,
            device_id=(me, tp_other), device_id_type=MESH)

    barrier = pltpu.get_barrier_semaphore()
    for k in range(1, n):
        pl.semaphore_signal(
            barrier, inc=1, device_id=(lax.rem(me + k, n), tp), device_id_type=MESH)
    pl.semaphore_signal(barrier, inc=1, device_id=(me, tp_other), device_id_type=MESH)
    kv[0, 0] = k_ref[...]
    kv[0, 1] = v_ref[...]
    for r in range(1, window):
        @pl.when(me < r)
        def _():
            kv[r] = jnp.zeros(kv.shape[1:], kv.dtype)

    @pl.when(me == 0)
    def _():
        q_rim[...] = jnp.zeros(q_rim.shape, q_rim.dtype)
        bc_rim[...] = jnp.zeros(bc_rim.shape, bc_rim.dtype)

    steps = step_ref[...]
    for d in range(n):
        dt_own[d, 0:2] = steps[2 * d:2 * d + 2]

    pl.semaphore_wait(barrier, n)

    half = window // 2
    direct = []
    for k in range(1, half + 1):
        copy = to_ctx(kv.at[0], kv.at[2 * k], kv_send.at[k], kv_recv.at[2 * k],
                      jnp.minimum(me + 2 * k, n - 1))
        wanted = me + 2 * k < n
        if 2 * k >= window:
            wanted = wanted & (parity == 1)
        direct.append((wanted, copy))
    even = parity == 0
    odd = parity == 1
    relay_even = [to_ctx(kv.at[r], kv.at[r + 1], kv_send.at[half + 1 + r], kv_recv.at[r + 1], pair)
                  for r in range(0, window, 2)]
    relay_odd = [to_ctx(kv.at[r], kv.at[r - 1], kv_send.at[half + 1 + r], kv_recv.at[r - 1], pair)
                 for r in range(2, window + 1, 2)]
    nxt = jnp.minimum(me + 1, n - 1)
    rim_q = to_ctx(q_ref.at[pl.ds(rows - RIM, RIM)], q_rim, rim_send.at[0], rim_recv.at[0], nxt)
    rim_b = to_ctx(bc_ref.at[pl.ds(rows - RIM, RIM)], bc_rim, rim_send.at[1], rim_recv.at[1], nxt)

    @pl.when(me + 1 < n)
    def _():
        rim_b.start()

    @pl.when(even)
    def _():
        relay_even[0].start()

    for wanted, copy in direct:
        @pl.when(wanted)
        def _():
            copy.start()

    @pl.when(me + 1 < n)
    def _():
        rim_q.start()

    for k in range(1, n):
        d = lax.rem(me + k, n)
        to_ctx(dt_own.at[d], dt_all.at[me], dt_send.at[k], dt_recv.at[me], d).start()
    dt_all[me] = dt_own[me]

    starts = []
    total = jnp.int32(0)
    for i in range(ndoc):
        starts.append(total)
        total = total + doc_ref[i]

    def first_of(pos):
        first = jnp.zeros_like(pos)
        for s in starts:
            first = jnp.where(s <= pos, s, first)
        return first

    row_iota = lax.broadcasted_iota(jnp.int32, (rows, LANES), 0)
    lane_iota = lax.broadcasted_iota(jnp.int32, (rows, LANES), 1)
    base = me * rows
    own_pos = base + row_iota
    own_first = first_of(own_pos)
    tap_count = taps_ref.shape[0]
    since = own_pos - own_first

    def conv(extended, taps):
        acc = None
        for m in range(tap_count):
            part = extended[8 - m: 8 - m + rows] * taps[tap_count - 1 - m: tap_count - m]
            part = jnp.where(since >= m, part, 0.0)
            acc = part if acc is None else acc + part
        return silu(acc).astype(jnp.bfloat16)

    @pl.when(me > 0)
    def _():
        rim_b.wait_recv()

    for i in range(2):
        for piece in range(state_size // LANES):
            cols = pl.ds(pl.multiple_of(
                (i * groups + group) * state_size + piece * LANES, LANES), LANES)
            extended = jnp.concatenate(
                [bc_rim[:, cols].astype(jnp.float32)[RIM - 8:], bc_ref[:, cols].astype(jnp.float32)], axis=0)
            lanes = slice(piece * LANES, (piece + 1) * LANES)
            taps = jnp.zeros((tap_count, LANES), jnp.float32)
            for g in range(groups):
                part = jnp.concatenate(
                    [bc_taps_ref[m, i, g:g + 1, lanes] for m in range(tap_count)], axis=0)
                taps = jnp.where(group == g, part, taps)
            bc_all[me, i, :, piece * LANES:(piece + 1) * LANES] = conv(extended, taps)

    column = [lax.rem(me + 2 * k, n) for k in range(1, n // 2)]

    def relay_bc(s, slot):
        return to_ctx(bc_all.at[s, core], bc_all.at[s, core], bc_send.at[slot], bc_recv.at[s], pair)

    def share_bc(s, slot):
        return to_core(bc_all.at[s, core], bc_all.at[s, core], bc_core_send.at[slot], bc_core_recv.at[s])

    bc_own = [to_ctx(bc_all.at[me, core], bc_all.at[me, core], bc_send.at[0], bc_recv.at[me], pair)]
    for k, d in enumerate(column):
        bc_own.append(to_ctx(bc_all.at[me, core], bc_all.at[me, core],
                             bc_send.at[1 + k], bc_recv.at[me], d))

    for r in range(2, window + 1, 2):
        cond = me >= r
        if r >= window:
            cond = cond & odd

        @pl.when(cond)
        def _():
            to_ctx(kv.at[0], kv.at[r], kv_send.at[0], kv_recv.at[r], pair).wait_recv()

        if r < window:
            @pl.when(even & (me >= r))
            def _():
                relay_even[r // 2].start()

        @pl.when(odd & (me >= r))
        def _():
            relay_odd[r // 2 - 1].start()
    for copy in bc_own:
        copy.start()
    for r in range(1, window, 2):
        @pl.when(me >= r)
        def _():
            to_ctx(kv.at[0], kv.at[r], kv_send.at[0], kv_recv.at[r], pair).wait_recv()

    @pl.when(me > 0)
    def _():
        rim_q.wait_recv()

    keys = jnp.concatenate([kv[r, 0] for r in range(window)], axis=0)
    values = jnp.concatenate([kv[r, 1] for r in range(window)], axis=0)
    values = jnp.concatenate([values, jnp.ones_like(values)], axis=1)
    scale = math.log2(math.e) / math.sqrt(k_ref.shape[1])

    def bias_of(pos):
        first = first_of(pos)
        parts = []
        for r in range(window):
            key_pos = (me - r) * rows + lane_iota
            parts.append(jnp.where((key_pos <= pos) & (key_pos >= first), 0.0, NEGATIVE_FILL))
        return jnp.concatenate(parts, axis=1)

    def attention(block, bias):
        scores = dot_nt(block, keys) + bias
        exponent = jnp.exp2((scores - jnp.max(scores, axis=1, keepdims=True)) * scale)
        summed = dot_nn(exponent.astype(jnp.bfloat16), values)
        return (summed[:, :LANES] / summed[:, LANES:]).astype(jnp.bfloat16).astype(jnp.float32)

    rim_block = jnp.concatenate(
        [q_rim[:, h * LANES:(h + 1) * LANES] for h in range(n)], axis=0)
    rim_pos = base - RIM + lax.rem(row_iota, RIM)
    gated_ref[0] = attention(rim_block, bias_of(rim_pos))
    bias = bias_of(own_pos)

    def recv_bc(s):
        to_ctx(bc_all.at[s, core], bc_all.at[s, core], bc_send.at[0], bc_recv.at[s], pair).wait_recv()

    for k in range(n):
        h = lax.rem(me + 1 + k, n)
        cols = pl.ds(pl.multiple_of(h * LANES, LANES), LANES)
        attended = attention(q_ref[:, cols], bias)
        rim = gated_ref[0, pl.ds(pl.multiple_of(h * RIM + RIM - 8, 8), 8), :]
        x = conv(jnp.concatenate([rim, attended], axis=0), taps_ref[:, cols])
        if k < n - 1:
            x_out[h] = x
            to_ctx(x_out.at[h], x_all.at[me], x_send.at[k], x_recv.at[me], h).start()
        else:
            x_all[me] = x
        if k >= n // 2 and k - n // 2 < len(column):
            s = column[k - n // 2]
            recv_bc(s)
            relay_bc(s, n // 2 + k - n // 2).start()
            share_bc(s, k - n // 2).start()
    crossed = [pair] + [lax.rem(pair + 2 * k, n) for k in range(1, n // 2)]
    for k, s in enumerate(crossed):
        recv_bc(s)
        share_bc(s, n // 2 - 1 + k).start()

    upper = (row_iota <= lane_iota).astype(jnp.float32)
    left = lane_iota < LANES // 2
    rate = [rate_ref[2 * me + a] for a in range(2)]
    skip = jnp.where(left[:1], skip_ref[2 * me], skip_ref[2 * me + 1])
    for k in range(1, n):
        s = lax.rem(me + k, n)
        to_ctx(dt_own.at[s], dt_all.at[s], dt_send.at[k], dt_recv.at[s], s).wait_recv()
    dt_rows = [jnp.concatenate([dt_all[i, a:a + 1] for i in range(n)], axis=0) for a in range(2)]
    cum_rows = [jnp.dot(-rate[a] * dt_rows[a], upper, precision=lax.Precision.HIGHEST,
                        preferred_element_type=jnp.float32) for a in range(2)]
    keeps = []
    for i in range(n):
        @pl.when(me != i)
        def _():
            other = 1 - core
            to_core(bc_all.at[i, other], bc_all.at[i, other], bc_core_send.at[0],
                    bc_core_recv.at[i]).wait_recv()

        start = i * rows
        pos = start + row_iota
        first = first_of(pos)
        key_pos = start + lane_iota
        visible = (key_pos >= first) & (key_pos <= pos)
        cum = [cum_rows[a][i:i + 1] for a in range(2)]
        dts = [dt_rows[a][i:i + 1] for a in range(2)]
        side = (rows // 2, LANES)
        cum_col = jnp.concatenate([jnp.broadcast_to(r, side) for r in cum], axis=0).T
        dt_col = jnp.concatenate([jnp.broadcast_to(r, side) for r in dts], axis=0).T
        gram = jnp.where(visible, dot_nt(bc_all[i, 1], bc_all[i, 0]), 0.0)
        for a in range(2):
            col = cum_col[:, a * (LANES // 2):a * (LANES // 2) + 1]
            gap = jnp.where(visible, col - cum[a], 0.0)
            mix_ref[i, :, a * LANES:(a + 1) * LANES] = (
                gram * jnp.exp(gap) * dts[a]).astype(jnp.bfloat16)
        last_start = first[rows - 1:rows]
        cum_last = cum_col[rows - 1:rows]
        carry_ref[i] = jnp.where(first < start, jnp.exp(cum_col), 0.0)
        weight_ref[i] = jnp.where(pos >= last_start, jnp.exp(cum_last - cum_col) * dt_col, 0.0)
        keeps.append(jnp.where(last_start < start, jnp.exp(cum_last), 0.0))

    state = jnp.zeros((state_size, LANES), jnp.float32)
    for i in range(n):
        @pl.when(me != i)
        def _():
            to_ctx(x_all.at[i], x_all.at[i], x_send.at[0], x_recv.at[i], pair).wait_recv()

        state_ref[i] = state.astype(jnp.bfloat16)
        if i < n - 1:
            weighted = (x_all[i].astype(jnp.float32) * weight_ref[i]).astype(jnp.bfloat16)
            state = keeps[i] * state + dot_tn(bc_all[i, 0], weighted)

    for k in range(n):
        i = lax.rem(me + 1 + k, n)
        xw = x_all[i].astype(jnp.float32)
        both = jnp.concatenate([jnp.where(left, xw, 0.0), jnp.where(left, 0.0, xw)], axis=0)
        y = dot_nn(mix_ref[i], both.astype(jnp.bfloat16)) + skip * xw
        y = (y + carry_ref[i] * dot_nn(bc_all[i, 1], state_ref[i])).astype(jnp.bfloat16)
        if k < n - 1:
            y_out[i] = y
            to_ctx(y_out.at[i], y_all.at[me], y_send.at[i], y_recv.at[me], i).start()
        else:
            y_all[me] = y

    squares = jnp.zeros((rows, LANES), jnp.float32)
    for k in range(n):
        h = lax.rem(me + n - 1 - k, n)
        if k < n - 1:
            to_ctx(y_out.at[h], y_all.at[h], y_send.at[h], y_recv.at[h], h).wait_recv()
        z = gate_ref[:, pl.ds(pl.multiple_of(h * LANES, LANES), LANES)].astype(jnp.float32)
        gated = y_all[h].astype(jnp.float32) * silu(z)
        gated_ref[h] = gated
        squares = squares + gated * gated
    sq_own[...] = squares
    swap = to_core(sq_own, sq_other, sq_sem.at[0], sq_sem.at[1])
    swap.start()

    for wanted, copy in direct:
        @pl.when(wanted)
        def _():
            copy.wait_send()
    for j, r in enumerate(range(0, window, 2)):
        @pl.when(even & (me >= r))
        def _():
            relay_even[j].wait_send()
    for j, r in enumerate(range(2, window + 1, 2)):
        @pl.when(odd & (me >= r))
        def _():
            relay_odd[j].wait_send()

    @pl.when(me + 1 < n)
    def _():
        rim_q.wait_send()
        rim_b.wait_send()
    for copy in bc_own:
        copy.wait_send()
    for k, s in enumerate(column):
        relay_bc(s, n // 2 + k).wait_send()
        share_bc(s, k).wait_send()
    for k, s in enumerate(crossed):
        share_bc(s, n // 2 - 1 + k).wait_send()
    for k in range(n - 1):
        h = lax.rem(me + 1 + k, n)
        to_ctx(x_out.at[h], x_all.at[me], x_send.at[k], x_recv.at[me], h).wait_send()
        to_ctx(dt_own.at[h], dt_all.at[me], dt_send.at[k + 1], dt_recv.at[me], h).wait_send()
    for i in range(n):
        @pl.when(me != i)
        def _():
            to_ctx(y_out.at[i], y_all.at[me], y_send.at[i], y_recv.at[me], i).wait_send()
    swap.wait()
    width = 2 * n * LANES
    mean_square = jnp.sum(sq_own[...] + sq_other[...], axis=1, keepdims=True) / width
    factor = lax.rsqrt(mean_square + EPSILON)
    for h in range(n):
        cols = slice(h * LANES, (h + 1) * LANES)
        out_ref[:, cols] = (gated_ref[h] * factor * gain_ref[:, cols]).astype(jnp.bfloat16)


def fused_on_device(
    queries, key_rows, value_rows, doc_lengths, gate_input, bc_input, step_size,
    decay_rate, skip_gain, conv_x, conv_bc, norm_gain,
):
    n = lax.axis_size("ctx")
    rows = queries.shape[0]
    state_size = bc_input.shape[3]
    longest = n * rows // 2 + 64
    window = 1 + -(-(longest - 1) // rows)
    bc = bc_input.reshape(rows, -1)
    bf16, f32 = jnp.bfloat16, jnp.float32
    vmem = pl.BlockSpec(memory_space=pltpu.VMEM)
    smem = pl.BlockSpec(memory_space=pltpu.SMEM)
    dma = pltpu.SemaphoreType.DMA
    half = window // 2
    return pl.pallas_call(
        functools.partial(fused_kernel, n, window),
        out_shape=jax.ShapeDtypeStruct(queries.shape, bf16),
        in_specs=[smem] * 3 + [vmem] * 9,
        out_specs=vmem,
        scratch_shapes=[
            pltpu.VMEM((window + 1, 2, rows, LANES), bf16),
            pltpu.VMEM((RIM, queries.shape[1]), bf16),
            pltpu.VMEM((RIM, bc.shape[1]), bf16),
            pltpu.VMEM((n, 2, rows, state_size), bf16),
            pltpu.VMEM((n, rows, LANES), bf16),
            pltpu.VMEM((n, rows, LANES), bf16),
            pltpu.VMEM((n, 8, LANES), f32),
            pltpu.VMEM((n, 8, LANES), f32),
            pltpu.VMEM((n, rows, 2 * LANES), bf16),
            pltpu.VMEM((n, rows, LANES), f32),
            pltpu.VMEM((n, rows, LANES), f32),
            pltpu.VMEM((n, state_size, LANES), bf16),
            pltpu.VMEM((n, rows, LANES), bf16),
            pltpu.VMEM((n, rows, LANES), bf16),
            pltpu.VMEM((n, rows, LANES), f32),
            pltpu.VMEM((rows, LANES), f32),
            pltpu.VMEM((rows, LANES), f32),
            dma((half + 2 + window,)),
            dma((window + 1,)),
            dma((2,)),
            dma((2,)),
            dma((n,)),
            dma((n,)),
            dma((n,)),
            dma((n,)),
            dma((n,)),
            dma((n,)),
            dma((n,)),
            dma((n,)),
            dma((n,)),
            dma((n,)),
            dma((2,)),
        ],
        compiler_params=pltpu.CompilerParams(
            collective_id=0, has_side_effects=True, vmem_limit_bytes=32 * 1024 * 1024),
    )(
        doc_lengths, decay_rate, skip_gain, queries, key_rows, value_rows, gate_input, bc, step_size.T,
        conv_x, conv_bc, norm_gain.reshape(1, -1),
    )


def plan(queries, key_rows, *rest):
    blocks = queries.shape[1] // LANES
    if blocks == lax.axis_size("ctx") and queries.shape[0] == LANES:
        return fused_on_device(queries, key_rows, *rest)
    return on_device(queries, key_rows, *rest)


def solution(mesh):
    return jax.shard_map(
        plan,
        mesh=mesh,
        in_specs=(
            P("ctx", "tp"),
            P("ctx", "tp"),
            P("ctx", "tp"),
            P(),
            P("ctx", "tp"),
            P("ctx", None, None, None),
            P("ctx", "tp"),
            P("tp"),
            P("tp"),
            P(None, "tp"),
            P(),
            P("tp"),
        ),
        out_specs=P("ctx", "tp"),
        check_vma=False,
    )
```

```python
import functools
import math

import jax
import jax.numpy as jnp
from jax import lax
from jax.experimental import pallas as pl
from jax.experimental.pallas import tpu as pltpu
from jax.sharding import PartitionSpec as P

EPSILON = 1e-05
NEGATIVE_FILL = -1e30


def from_behind(x, axis, by):
    size = lax.axis_size(axis)
    pairs = [(i, i + by) for i in range(size) if 0 <= i + by < size]
    return lax.ppermute(x, axis, pairs)


def prefix(x, axis, combine, identity):
    size, mine = (lax.axis_size(axis), lax.axis_index(axis))
    everything = jax.tree.map(
        lambda part, kind: lax.all_gather(part.astype(kind), axis), x, (jnp.bfloat16, jnp.bfloat16)
    )
    start = jax.tree.map(
        lambda part, zero: jnp.broadcast_to(jnp.asarray(zero, part.dtype), part.shape), x, identity
    )

    def step(k, before):
        reached = k < mine
        new = combine(
            before, jax.tree.map(lambda part, own: part[k].astype(own.dtype), everything, x)
        )
        return jax.tree.map(lambda a, b: jnp.where(reached, a, b), new, before)

    return lax.fori_loop(0, size, step, start)


def swapped(block, axis, bit):
    count = lax.axis_size(axis)
    route = []
    for low in range(count):
        high = low | 1 << bit
        if high != low and high < count:
            route += [(low, high), (high, low)]
    return lax.ppermute(block, axis, route)


def first_positions(doc_lengths, positions):
    doc_ends = jnp.cumsum(doc_lengths)
    doc_starts = doc_ends - doc_lengths
    covered = doc_starts[None, :] <= positions[:, None]
    return jnp.max(
        jnp.where(covered, doc_starts[None, :], jnp.zeros_like(doc_starts)[None, :]), axis=1
    )


def attend(
    running, key_block, value_block, key_start, query_rows, query_pos, query_first, score_scale
):
    maximum, totals, summed = running
    key_pos = key_start + jnp.arange(key_block.shape[0], dtype=jnp.int32)
    scores = (
        jnp.einsum("qhd,kd->hqk", query_rows, key_block, preferred_element_type=jnp.float32)
        * score_scale
    )
    visible = (
        (key_pos[None, :] <= query_pos[:, None]) & (key_pos[None, :] >= query_first[:, None])
    )[None]
    masked = jnp.where(visible, scores, NEGATIVE_FILL)
    new_maximum = jnp.maximum(maximum, jnp.max(masked, axis=-1))
    exponent = jnp.where(visible, jnp.exp(masked - new_maximum[..., None]), 0.0)
    factor = jnp.exp(maximum - new_maximum)
    totals = totals * factor + jnp.sum(exponent, axis=-1)
    weights = exponent.astype(jnp.bfloat16)
    summed = summed * factor[..., None] + jnp.einsum(
        "hqk,kd->hqd", weights, value_block, preferred_element_type=jnp.float32
    )
    return (new_maximum, totals, summed)


def key_folder(query_rows, query_pos, query_first, score_scale):
    query_last = jnp.max(query_pos)
    earliest = jnp.min(query_first)

    def maybe_attend(running, key_slab, value_slab, key_start):
        needed = (key_start <= query_last) & (key_start + key_slab.shape[0] > earliest)

        def compute(inner_run):
            return attend(
                inner_run,
                key_slab,
                value_slab,
                key_start,
                query_rows,
                query_pos,
                query_first,
                score_scale,
            )

        def keep(inner_run):
            return inner_run

        return lax.cond(needed, compute, keep, running)

    def fold_keys(running, pieces, offset):
        key_block, value_block = pieces
        key_count = key_block.shape[0]
        block_width = 256
        block_count = key_count // block_width

        def visit(inner_run, entries):
            block_index, key_slab, value_slab = entries
            return (maybe_attend(inner_run, key_slab, value_slab, block_index * block_width), None)

        running, _ = lax.scan(
            visit,
            running,
            (
                jnp.arange(block_count, dtype=jnp.int32),
                key_block.reshape(block_count, block_width, -1),
                value_block.reshape(block_count, block_width, -1),
            ),
        )
        return running

    return fold_keys


def finish(running, row_count):
    maximum, totals, summed = running
    output = summed / totals[..., None]
    return jnp.transpose(output, (1, 0, 2)).reshape(row_count, -1).astype(jnp.bfloat16)


def causal_local(extended, taps, positions, first_token, tap_count):
    row_count = positions.shape[0]
    accumulated = jnp.zeros((row_count,) + extended.shape[1:], jnp.float32)
    for shift_by in range(tap_count):
        tap_rows = extended[tap_count - 1 - shift_by : tap_count - 1 - shift_by + row_count].astype(
            jnp.float32
        )
        usable = (positions - shift_by >= first_token).reshape(
            (row_count,) + (1,) * (extended.ndim - 1)
        )
        accumulated = accumulated + jnp.where(
            usable, tap_rows * taps[tap_count - 1 - shift_by], 0.0
        )
    return accumulated


def combine_states(earlier, following):
    return (earlier[0] * following[0], earlier[1] * following[0][:, None, None] + following[1])


def on_device(
    queries,
    key_rows,
    value_rows,
    doc_lengths,
    gate_input,
    bc_input,
    step_size,
    decay_rate,
    skip_gain,
    conv_x,
    conv_bc,
    norm_gain,
):
    row_count = queries.shape[0]
    head_size = key_rows.shape[1]
    head_count = queries.shape[1] // head_size
    score_scale = 1.0 / math.sqrt(head_size)
    ctx_index = lax.axis_index("ctx")
    block_start = ctx_index * row_count
    own_pos = block_start + jnp.arange(row_count, dtype=jnp.int32)
    own_first = first_positions(doc_lengths, own_pos)
    initial = (
        jnp.full((head_count, row_count), NEGATIVE_FILL, jnp.float32),
        jnp.zeros((head_count, row_count), jnp.float32),
        jnp.zeros((head_count, row_count, head_size), jnp.float32),
    )
    query_rows = queries.reshape(row_count, head_count, head_size)
    running = key_folder(query_rows, own_pos, own_first, score_scale)(
        initial,
        (
            lax.all_gather(key_rows, "ctx", axis=0, tiled=True),
            lax.all_gather(value_rows, "ctx", axis=0, tiled=True),
        ),
        jnp.int32(0),
    )
    attended = finish(running, row_count)
    group_index = lax.axis_index("tp") // 2
    bc_local = lax.dynamic_index_in_dim(bc_input, group_index, 2, keepdims=False)
    conv_bc_local = lax.dynamic_index_in_dim(conv_bc, group_index, 2, keepdims=False)
    tap_count = conv_x.shape[0]
    rim_input, rim_bc = from_behind(
        (attended[row_count - tap_count + 1 :], bc_local[row_count - tap_count + 1 :]), "ctx", 1
    )
    mixed_input = jax.nn.silu(
        causal_local(
            jnp.concatenate([rim_input, attended], 0), conv_x, own_pos, own_first, tap_count
        )
    ).astype(jnp.bfloat16)
    bc_conv = jax.nn.silu(
        causal_local(
            jnp.concatenate([rim_bc, bc_local], 0), conv_bc_local, own_pos, own_first, tap_count
        )
    ).astype(jnp.bfloat16)
    heads_local = step_size.shape[1]
    input_heads = mixed_input.reshape(row_count, heads_local, -1)
    b_values = bc_conv[:, 0]
    c_values = bc_conv[:, 1]
    highest = lax.Precision.HIGHEST
    log_decay = -decay_rate[None, :] * step_size
    cumulated = jnp.cumsum(log_decay, axis=0)
    gram_matrix = jnp.dot(c_values, b_values.T, preferred_element_type=jnp.float32)
    visible = (own_pos[None, :] >= own_first[:, None]) & (own_pos[None, :] <= own_pos[:, None])
    cum_heads = cumulated.T
    log_gap = jnp.where(visible[None], cum_heads[:, :, None] - cum_heads[:, None, :], -jnp.inf)
    mixing = gram_matrix[None] * jnp.exp(log_gap) * step_size.T[:, None, :]
    input_wide = input_heads.astype(jnp.float32)
    inner_part = jnp.einsum("hts,shp->thp", mixing, input_wide, precision=highest)
    last_start = own_first[-1]
    state_weight = jnp.where(
        (own_pos >= last_start)[:, None], jnp.exp(cumulated[-1][None, :] - cumulated), 0.0
    )
    state_weight = state_weight * step_size
    block_state = jnp.einsum(
        "shp,sn->hpn",
        state_weight[:, :, None] * input_wide,
        b_values.astype(jnp.float32),
        precision=highest,
    )
    carry_decay = jnp.where(last_start < block_start, jnp.exp(cumulated[-1]), 0.0)
    identity = (jnp.ones_like(carry_decay), jnp.zeros_like(block_state))
    _, incoming = prefix((carry_decay, block_state), "ctx", combine_states, identity)
    carry_in = (own_first < block_start).astype(jnp.float32)
    carried_part = jnp.einsum(
        "tn,hpn->thp", c_values.astype(jnp.float32), incoming, precision=highest
    )
    carried_part = carried_part * (jnp.exp(cumulated) * carry_in[:, None])[:, :, None]
    ssm_out = inner_part + carried_part + skip_gain[None, :, None] * input_wide
    gated = ssm_out.reshape(row_count, -1) * jax.nn.silu(gate_input.astype(jnp.float32))
    square_sum = jnp.sum(gated * gated, axis=1)
    partner_sum = swapped(square_sum, "tp", 0)
    mean_square = (square_sum + partner_sum) / (2 * gated.shape[1])
    return (gated * lax.rsqrt(mean_square + EPSILON)[:, None] * norm_gain[None, :]).astype(
        jnp.bfloat16
    )


LANES = 128
RIM = 16
MESH = pl.DeviceIdType.MESH


def dot_nt(a, b):
    return lax.dot_general(a, b, (((1,), (1,)), ((), ())), preferred_element_type=jnp.float32)


def dot_tn(a, b):
    return lax.dot_general(a, b, (((0,), (0,)), ((), ())), preferred_element_type=jnp.float32)


def dot_nn(a, b):
    return jnp.dot(a, b, preferred_element_type=jnp.float32)


def silu(v):
    return v / (1.0 + jnp.exp(-v))


def fused_kernel(
    n,
    window,
    doc_ref,
    rate_ref,
    skip_ref,
    q_in,
    k_in,
    v_in,
    gate_in,
    bc_in,
    step_in,
    taps_in,
    bc_taps_in,
    gain_in,
    out_ref,
    q_ref,
    gate_ref,
    bc_ref,
    step_ref,
    taps_ref,
    bc_taps_ref,
    gain_ref,
    load_sem,
    kv,
    q_rim,
    bc_rim,
    bc_all,
    x_out,
    x_all,
    dt_own,
    dt_all,
    mix_ref,
    weight_ref,
    carry_ref,
    state_ref,
    y_out,
    y_all,
    gated_ref,
    sq_own,
    sq_other,
    kv_send,
    kv_recv,
    rim_send,
    rim_recv,
    bc_send,
    bc_recv,
    bc_core_send,
    bc_core_recv,
    x_send,
    x_recv,
    dt_send,
    dt_recv,
    y_send,
    y_recv,
    sq_sem,
):
    loads = [
        pltpu.make_async_copy(src, dst, load_sem.at[i])
        for i, (src, dst) in enumerate((
            (k_in, kv.at[0, 0]), (v_in, kv.at[0, 1]), (bc_in, bc_ref), (q_in, q_ref),
            (step_in, step_ref), (bc_taps_in, bc_taps_ref), (taps_in, taps_ref),
            (gate_in, gate_ref), (gain_in, gain_ref)))
    ]
    for load in loads:
        load.start()
    rows = q_ref.shape[0]
    me = lax.axis_index("ctx")
    tp = lax.axis_index("tp")
    core = lax.rem(tp, 2)
    group = tp // 2
    tp_other = tp + 1 - 2 * core
    parity = lax.rem(me, 2)
    pair = me + 1 - 2 * parity
    state_size = bc_all.shape[3]
    ndoc = doc_ref.shape[0]
    groups = bc_ref.shape[1] // (2 * state_size)

    def to_ctx(src, dst, send, recv, where):
        return pltpu.make_async_remote_copy(
            src_ref=src, dst_ref=dst, send_sem=send, recv_sem=recv,
            device_id=(where, tp), device_id_type=MESH)

    def to_core(src, dst, send, recv):
        return pltpu.make_async_remote_copy(
            src_ref=src, dst_ref=dst, send_sem=send, recv_sem=recv,
            device_id=(me, tp_other), device_id_type=MESH)

    barrier = pltpu.get_barrier_semaphore()
    for k in range(1, n):
        pl.semaphore_signal(
            barrier, inc=1, device_id=(lax.rem(me + k, n), tp), device_id_type=MESH)
    pl.semaphore_signal(barrier, inc=1, device_id=(me, tp_other), device_id_type=MESH)
    for r in range(1, window):
        @pl.when(me < r)
        def _():
            kv[r] = jnp.zeros(kv.shape[1:], kv.dtype)

    @pl.when(me == 0)
    def _():
        q_rim[...] = jnp.zeros(q_rim.shape, q_rim.dtype)
        bc_rim[...] = jnp.zeros(bc_rim.shape, bc_rim.dtype)

    for load in loads:
        load.wait()
    steps = step_ref[...]
    for d in range(n):
        dt_own[d, 0:2] = steps[2 * d:2 * d + 2]

    pl.semaphore_wait(barrier, n)

    half = window // 2
    direct = []
    for k in range(1, half + 1):
        copy = to_ctx(kv.at[0], kv.at[2 * k], kv_send.at[k], kv_recv.at[2 * k],
                      jnp.minimum(me + 2 * k, n - 1))
        wanted = me + 2 * k < n
        if 2 * k >= window:
            wanted = wanted & (parity == 1)
        direct.append((wanted, copy))
    even = parity == 0
    odd = parity == 1
    relay_even = [to_ctx(kv.at[r], kv.at[r + 1], kv_send.at[half + 1 + r], kv_recv.at[r + 1], pair)
                  for r in range(0, window, 2)]
    relay_odd = [to_ctx(kv.at[r], kv.at[r - 1], kv_send.at[half + 1 + r], kv_recv.at[r - 1], pair)
                 for r in range(2, window + 1, 2)]
    nxt = jnp.minimum(me + 1, n - 1)
    rim_q = to_ctx(q_ref.at[pl.ds(rows - RIM, RIM)], q_rim, rim_send.at[0], rim_recv.at[0], nxt)
    rim_b = to_ctx(bc_ref.at[pl.ds(rows - RIM, RIM)], bc_rim, rim_send.at[1], rim_recv.at[1], nxt)

    @pl.when(me + 1 < n)
    def _():
        rim_b.start()

    @pl.when(even)
    def _():
        relay_even[0].start()

    for wanted, copy in direct:
        @pl.when(wanted)
        def _():
            copy.start()

    @pl.when(me + 1 < n)
    def _():
        rim_q.start()

    for k in range(1, n):
        d = lax.rem(me + k, n)
        to_ctx(dt_own.at[d], dt_all.at[me], dt_send.at[k], dt_recv.at[me], d).start()
    dt_all[me] = dt_own[me]

    starts = []
    total = jnp.int32(0)
    for i in range(ndoc):
        starts.append(total)
        total = total + doc_ref[i]

    def first_of(pos):
        first = jnp.zeros_like(pos)
        for s in starts:
            first = jnp.where(s <= pos, s, first)
        return first

    row_iota = lax.broadcasted_iota(jnp.int32, (rows, LANES), 0)
    lane_iota = lax.broadcasted_iota(jnp.int32, (rows, LANES), 1)
    base = me * rows
    own_pos = base + row_iota
    own_first = first_of(own_pos)
    tap_count = taps_ref.shape[0]
    since = own_pos - own_first

    def conv(extended, taps):
        acc = None
        for m in range(tap_count):
            part = extended[8 - m: 8 - m + rows] * taps[tap_count - 1 - m: tap_count - m]
            part = jnp.where(since >= m, part, 0.0)
            acc = part if acc is None else acc + part
        return silu(acc).astype(jnp.bfloat16)

    @pl.when(me > 0)
    def _():
        rim_b.wait_recv()

    for i in range(2):
        for piece in range(state_size // LANES):
            cols = pl.ds(pl.multiple_of(
                (i * groups + group) * state_size + piece * LANES, LANES), LANES)
            extended = jnp.concatenate(
                [bc_rim[:, cols].astype(jnp.float32)[RIM - 8:], bc_ref[:, cols].astype(jnp.float32)], axis=0)
            lanes = slice(piece * LANES, (piece + 1) * LANES)
            taps = jnp.zeros((tap_count, LANES), jnp.float32)
            for g in range(groups):
                part = jnp.concatenate(
                    [bc_taps_ref[m, i, g:g + 1, lanes] for m in range(tap_count)], axis=0)
                taps = jnp.where(group == g, part, taps)
            bc_all[me, i, :, piece * LANES:(piece + 1) * LANES] = conv(extended, taps)

    column = [lax.rem(me + 2 * k, n) for k in range(1, n // 2)]

    def relay_bc(s, slot):
        return to_ctx(bc_all.at[s, core], bc_all.at[s, core], bc_send.at[slot], bc_recv.at[s], pair)

    def share_bc(s, slot):
        return to_core(bc_all.at[s, core], bc_all.at[s, core], bc_core_send.at[slot], bc_core_recv.at[s])

    bc_own = [to_ctx(bc_all.at[me, core], bc_all.at[me, core], bc_send.at[0], bc_recv.at[me], pair)]
    for k, d in enumerate(column):
        bc_own.append(to_ctx(bc_all.at[me, core], bc_all.at[me, core],
                             bc_send.at[1 + k], bc_recv.at[me], d))

    for r in range(2, window + 1, 2):
        cond = me >= r
        if r >= window:
            cond = cond & odd

        @pl.when(cond)
        def _():
            to_ctx(kv.at[0], kv.at[r], kv_send.at[0], kv_recv.at[r], pair).wait_recv()

        if r == 2:
            for copy in bc_own:
                copy.start()
        if r < window:
            @pl.when(even & (me >= r))
            def _():
                relay_even[r // 2].start()

        @pl.when(odd & (me >= r))
        def _():
            relay_odd[r // 2 - 1].start()
    for r in range(1, window, 2):
        @pl.when(me >= r)
        def _():
            to_ctx(kv.at[0], kv.at[r], kv_send.at[0], kv_recv.at[r], pair).wait_recv()

    @pl.when(me > 0)
    def _():
        rim_q.wait_recv()

    keys = jnp.concatenate([kv[r, 0] for r in range(window)], axis=0)
    values = jnp.concatenate([kv[r, 1] for r in range(window)], axis=0)
    values = jnp.concatenate([values, jnp.ones_like(values)], axis=1)
    scale = math.log2(math.e) / math.sqrt(k_in.shape[1])

    def bias_of(pos):
        first = first_of(pos)
        parts = []
        for r in range(window):
            key_pos = (me - r) * rows + lane_iota
            parts.append(jnp.where((key_pos <= pos) & (key_pos >= first), 0.0, NEGATIVE_FILL))
        return jnp.concatenate(parts, axis=1)

    def attention(block, bias):
        scores = dot_nt(block, keys) + bias
        exponent = jnp.exp2((scores - jnp.max(scores, axis=1, keepdims=True)) * scale)
        summed = dot_nn(exponent.astype(jnp.bfloat16), values)
        return (summed[:, :LANES] / summed[:, LANES:]).astype(jnp.bfloat16).astype(jnp.float32)

    rim_block = jnp.concatenate(
        [q_rim[:, h * LANES:(h + 1) * LANES] for h in range(n)], axis=0)
    rim_pos = base - RIM + lax.rem(row_iota, RIM)
    gated_ref[0] = attention(rim_block, bias_of(rim_pos))
    bias = bias_of(own_pos)

    def recv_bc(s):
        to_ctx(bc_all.at[s, core], bc_all.at[s, core], bc_send.at[0], bc_recv.at[s], pair).wait_recv()

    crossed = [pair] + [lax.rem(pair + 2 * k, n) for k in range(1, n // 2)]
    for k in range(n):
        h = lax.rem(me + 1 + k, n)
        cols = pl.ds(pl.multiple_of(h * LANES, LANES), LANES)
        attended = attention(q_ref[:, cols], bias)
        rim = gated_ref[0, pl.ds(pl.multiple_of(h * RIM + RIM - 8, 8), 8), :]
        x = conv(jnp.concatenate([rim, attended], axis=0), taps_ref[:, cols])
        if k < n - 1:
            x_out[h] = x
            to_ctx(x_out.at[h], x_all.at[me], x_send.at[k], x_recv.at[me], h).start()
        else:
            x_all[me] = x
        if 1 <= k <= len(column):
            s = column[k - 1]
            recv_bc(s)
            relay_bc(s, n // 2 + k - 1).start()
            share_bc(s, k - 1).start()
        if n // 2 <= k:
            s = crossed[k - n // 2]
            recv_bc(s)
            share_bc(s, k - 1).start()

    upper = (row_iota <= lane_iota).astype(jnp.float32)
    left = lane_iota < LANES // 2
    rate = [rate_ref[2 * me + a] for a in range(2)]
    skip = jnp.where(left[:1], skip_ref[2 * me], skip_ref[2 * me + 1])
    for k in range(1, n):
        s = lax.rem(me + k, n)
        to_ctx(dt_own.at[s], dt_all.at[s], dt_send.at[k], dt_recv.at[s], s).wait_recv()
    dt_rows = [jnp.concatenate([dt_all[i, a:a + 1] for i in range(n)], axis=0) for a in range(2)]
    cum_rows = [jnp.dot(-rate[a] * dt_rows[a], upper, precision=lax.Precision.HIGHEST,
                        preferred_element_type=jnp.float32) for a in range(2)]
    keeps = []
    other = 1 - core
    for k in range(1, n):
        s = lax.rem(me + k, n)
        to_core(bc_all.at[s, other], bc_all.at[s, other], bc_core_send.at[0],
                bc_core_recv.at[s]).wait_recv()
    for i in range(n):
        start = i * rows
        pos = start + row_iota
        first = first_of(pos)
        key_pos = start + lane_iota
        visible = (key_pos >= first) & (key_pos <= pos)
        cum = [cum_rows[a][i:i + 1] for a in range(2)]
        dts = [dt_rows[a][i:i + 1] for a in range(2)]
        side = (rows // 2, LANES)
        cum_col = jnp.concatenate([jnp.broadcast_to(r, side) for r in cum], axis=0).T
        dt_col = jnp.concatenate([jnp.broadcast_to(r, side) for r in dts], axis=0).T
        gram = jnp.where(visible, dot_nt(bc_all[i, 1], bc_all[i, 0]), 0.0)
        for a in range(2):
            col = cum_col[:, a * (LANES // 2):a * (LANES // 2) + 1]
            gap = jnp.where(visible, col - cum[a], 0.0)
            mix_ref[i, :, a * LANES:(a + 1) * LANES] = (
                gram * jnp.exp(gap) * dts[a]).astype(jnp.bfloat16)
        last_start = first[rows - 1:rows]
        cum_last = cum_col[rows - 1:rows]
        carry_ref[i] = jnp.where(first < start, jnp.exp(cum_col), 0.0)
        weight_ref[i] = jnp.where(pos >= last_start, jnp.exp(cum_last - cum_col) * dt_col, 0.0)
        keeps.append(jnp.where(last_start < start, jnp.exp(cum_last), 0.0))

    state = jnp.zeros((state_size, LANES), jnp.float32)
    for k in range(1, n):
        s = lax.rem(me + n - k, n)
        to_ctx(x_all.at[s], x_all.at[s], x_send.at[0], x_recv.at[s], pair).wait_recv()
    for i in range(n):
        state_ref[i] = state.astype(jnp.bfloat16)
        if i < n - 1:
            weighted = (x_all[i].astype(jnp.float32) * weight_ref[i]).astype(jnp.bfloat16)
            state = keeps[i] * state + dot_tn(bc_all[i, 0], weighted)

    for k in range(n):
        i = lax.rem(me + 1 + k, n)
        xw = x_all[i].astype(jnp.float32)
        both = jnp.concatenate([jnp.where(left, xw, 0.0), jnp.where(left, 0.0, xw)], axis=0)
        y = dot_nn(mix_ref[i], both.astype(jnp.bfloat16)) + skip * xw
        y = (y + carry_ref[i] * dot_nn(bc_all[i, 1], state_ref[i])).astype(jnp.bfloat16)
        if k < n - 1:
            y_out[i] = y
            to_ctx(y_out.at[i], y_all.at[me], y_send.at[i], y_recv.at[me], i).start()
        else:
            y_all[me] = y

    squares = jnp.zeros((rows, LANES), jnp.float32)
    for k in range(n):
        h = lax.rem(me + n - 1 - k, n)
        if k < n - 1:
            to_ctx(y_out.at[h], y_all.at[h], y_send.at[h], y_recv.at[h], h).wait_recv()
        z = gate_ref[:, pl.ds(pl.multiple_of(h * LANES, LANES), LANES)].astype(jnp.float32)
        gated = y_all[h].astype(jnp.float32) * silu(z)
        gated_ref[h] = gated
        squares = squares + gated * gated
    sq_own[...] = squares
    swap = to_core(sq_own, sq_other, sq_sem.at[0], sq_sem.at[1])
    swap.start()

    for wanted, copy in direct:
        @pl.when(wanted)
        def _():
            copy.wait_send()
    for j, r in enumerate(range(0, window, 2)):
        @pl.when(even & (me >= r))
        def _():
            relay_even[j].wait_send()
    for j, r in enumerate(range(2, window + 1, 2)):
        @pl.when(odd & (me >= r))
        def _():
            relay_odd[j].wait_send()

    @pl.when(me + 1 < n)
    def _():
        rim_q.wait_send()
        rim_b.wait_send()
    for copy in bc_own:
        copy.wait_send()
    for k, s in enumerate(column):
        relay_bc(s, n // 2 + k).wait_send()
        share_bc(s, k).wait_send()
    for k, s in enumerate(crossed):
        share_bc(s, n // 2 - 1 + k).wait_send()
    for k in range(n - 1):
        h = lax.rem(me + 1 + k, n)
        to_ctx(x_out.at[h], x_all.at[me], x_send.at[k], x_recv.at[me], h).wait_send()
        to_ctx(dt_own.at[h], dt_all.at[me], dt_send.at[k + 1], dt_recv.at[me], h).wait_send()
    for i in range(n):
        @pl.when(me != i)
        def _():
            to_ctx(y_out.at[i], y_all.at[me], y_send.at[i], y_recv.at[me], i).wait_send()
    swap.wait()
    width = 2 * n * LANES
    mean_square = jnp.sum(sq_own[...] + sq_other[...], axis=1, keepdims=True) / width
    factor = lax.rsqrt(mean_square + EPSILON)
    for h in range(n):
        cols = slice(h * LANES, (h + 1) * LANES)
        out_ref[:, cols] = (gated_ref[h] * factor * gain_ref[:, cols]).astype(jnp.bfloat16)


def fused_on_device(
    queries, key_rows, value_rows, doc_lengths, gate_input, bc_input, step_size,
    decay_rate, skip_gain, conv_x, conv_bc, norm_gain,
):
    n = lax.axis_size("ctx")
    rows = queries.shape[0]
    state_size = bc_input.shape[3]
    longest = n * rows // 2 + 64
    window = 1 + -(-(longest - 1) // rows)
    bc = bc_input.reshape(rows, -1)
    bf16, f32 = jnp.bfloat16, jnp.float32
    vmem = pl.BlockSpec(memory_space=pltpu.VMEM)
    smem = pl.BlockSpec(memory_space=pltpu.SMEM)
    dma = pltpu.SemaphoreType.DMA
    half = window // 2
    return pl.pallas_call(
        functools.partial(fused_kernel, n, window),
        out_shape=jax.ShapeDtypeStruct(queries.shape, bf16),
        in_specs=[smem] * 3 + [pl.BlockSpec(memory_space=pl.ANY)] * 9,
        out_specs=vmem,
        scratch_shapes=[
            pltpu.VMEM(queries.shape, bf16),
            pltpu.VMEM(gate_input.shape, bf16),
            pltpu.VMEM(bc.shape, bf16),
            pltpu.VMEM(step_size.shape[::-1], f32),
            pltpu.VMEM(conv_x.shape, f32),
            pltpu.VMEM(conv_bc.shape, f32),
            pltpu.VMEM((1, norm_gain.shape[0]), f32),
            dma((9,)),
            pltpu.VMEM((window + 1, 2, rows, LANES), bf16),
            pltpu.VMEM((RIM, queries.shape[1]), bf16),
            pltpu.VMEM((RIM, bc.shape[1]), bf16),
            pltpu.VMEM((n, 2, rows, state_size), bf16),
            pltpu.VMEM((n, rows, LANES), bf16),
            pltpu.VMEM((n, rows, LANES), bf16),
            pltpu.VMEM((n, 8, LANES), f32),
            pltpu.VMEM((n, 8, LANES), f32),
            pltpu.VMEM((n, rows, 2 * LANES), bf16),
            pltpu.VMEM((n, rows, LANES), f32),
            pltpu.VMEM((n, rows, LANES), f32),
            pltpu.VMEM((n, state_size, LANES), bf16),
            pltpu.VMEM((n, rows, LANES), bf16),
            pltpu.VMEM((n, rows, LANES), bf16),
            pltpu.VMEM((n, rows, LANES), f32),
            pltpu.VMEM((rows, LANES), f32),
            pltpu.VMEM((rows, LANES), f32),
            dma((half + 2 + window,)),
            dma((window + 1,)),
            dma((2,)),
            dma((2,)),
            dma((n,)),
            dma((n,)),
            dma((n,)),
            dma((n,)),
            dma((n,)),
            dma((n,)),
            dma((n,)),
            dma((n,)),
            dma((n,)),
            dma((n,)),
            dma((2,)),
        ],
        compiler_params=pltpu.CompilerParams(
            collective_id=0, has_side_effects=True, vmem_limit_bytes=58 * 1024 * 1024),
    )(
        doc_lengths, decay_rate, skip_gain, queries, key_rows, value_rows, gate_input, bc, step_size.T,
        conv_x, conv_bc, norm_gain.reshape(1, -1),
    )


def plan(queries, key_rows, *rest):
    blocks = queries.shape[1] // LANES
    if blocks == lax.axis_size("ctx") and queries.shape[0] == LANES:
        return fused_on_device(queries, key_rows, *rest)
    return on_device(queries, key_rows, *rest)


def solution(mesh):
    return jax.shard_map(
        plan,
        mesh=mesh,
        in_specs=(
            P("ctx", "tp"),
            P("ctx", "tp"),
            P("ctx", "tp"),
            P(),
            P("ctx", "tp"),
            P("ctx", None, None, None),
            P("ctx", "tp"),
            P("tp"),
            P("tp"),
            P(None, "tp"),
            P(),
            P("tp"),
        ),
        out_specs=P("ctx", "tp"),
        check_vma=False,
    )
```

```python
import functools
import math

import jax
import jax.numpy as jnp
from jax import lax
from jax.experimental import pallas as pl
from jax.experimental.pallas import tpu as pltpu
from jax.sharding import PartitionSpec as P

EPSILON = 1e-05
NEGATIVE_FILL = -1e30


def from_behind(x, axis, by):
    size = lax.axis_size(axis)
    pairs = [(i, i + by) for i in range(size) if 0 <= i + by < size]
    return lax.ppermute(x, axis, pairs)


def prefix(x, axis, combine, identity):
    size, mine = (lax.axis_size(axis), lax.axis_index(axis))
    everything = jax.tree.map(
        lambda part, kind: lax.all_gather(part.astype(kind), axis), x, (jnp.bfloat16, jnp.bfloat16)
    )
    start = jax.tree.map(
        lambda part, zero: jnp.broadcast_to(jnp.asarray(zero, part.dtype), part.shape), x, identity
    )

    def step(k, before):
        reached = k < mine
        new = combine(
            before, jax.tree.map(lambda part, own: part[k].astype(own.dtype), everything, x)
        )
        return jax.tree.map(lambda a, b: jnp.where(reached, a, b), new, before)

    return lax.fori_loop(0, size, step, start)


def swapped(block, axis, bit):
    count = lax.axis_size(axis)
    route = []
    for low in range(count):
        high = low | 1 << bit
        if high != low and high < count:
            route += [(low, high), (high, low)]
    return lax.ppermute(block, axis, route)


def first_positions(doc_lengths, positions):
    doc_ends = jnp.cumsum(doc_lengths)
    doc_starts = doc_ends - doc_lengths
    covered = doc_starts[None, :] <= positions[:, None]
    return jnp.max(
        jnp.where(covered, doc_starts[None, :], jnp.zeros_like(doc_starts)[None, :]), axis=1
    )


def attend(
    running, key_block, value_block, key_start, query_rows, query_pos, query_first, score_scale
):
    maximum, totals, summed = running
    key_pos = key_start + jnp.arange(key_block.shape[0], dtype=jnp.int32)
    scores = (
        jnp.einsum("qhd,kd->hqk", query_rows, key_block, preferred_element_type=jnp.float32)
        * score_scale
    )
    visible = (
        (key_pos[None, :] <= query_pos[:, None]) & (key_pos[None, :] >= query_first[:, None])
    )[None]
    masked = jnp.where(visible, scores, NEGATIVE_FILL)
    new_maximum = jnp.maximum(maximum, jnp.max(masked, axis=-1))
    exponent = jnp.where(visible, jnp.exp(masked - new_maximum[..., None]), 0.0)
    factor = jnp.exp(maximum - new_maximum)
    totals = totals * factor + jnp.sum(exponent, axis=-1)
    weights = exponent.astype(jnp.bfloat16)
    summed = summed * factor[..., None] + jnp.einsum(
        "hqk,kd->hqd", weights, value_block, preferred_element_type=jnp.float32
    )
    return (new_maximum, totals, summed)


def key_folder(query_rows, query_pos, query_first, score_scale):
    query_last = jnp.max(query_pos)
    earliest = jnp.min(query_first)

    def maybe_attend(running, key_slab, value_slab, key_start):
        needed = (key_start <= query_last) & (key_start + key_slab.shape[0] > earliest)

        def compute(inner_run):
            return attend(
                inner_run,
                key_slab,
                value_slab,
                key_start,
                query_rows,
                query_pos,
                query_first,
                score_scale,
            )

        def keep(inner_run):
            return inner_run

        return lax.cond(needed, compute, keep, running)

    def fold_keys(running, pieces, offset):
        key_block, value_block = pieces
        key_count = key_block.shape[0]
        block_width = 256
        block_count = key_count // block_width

        def visit(inner_run, entries):
            block_index, key_slab, value_slab = entries
            return (maybe_attend(inner_run, key_slab, value_slab, block_index * block_width), None)

        running, _ = lax.scan(
            visit,
            running,
            (
                jnp.arange(block_count, dtype=jnp.int32),
                key_block.reshape(block_count, block_width, -1),
                value_block.reshape(block_count, block_width, -1),
            ),
        )
        return running

    return fold_keys


def finish(running, row_count):
    maximum, totals, summed = running
    output = summed / totals[..., None]
    return jnp.transpose(output, (1, 0, 2)).reshape(row_count, -1).astype(jnp.bfloat16)


def causal_local(extended, taps, positions, first_token, tap_count):
    row_count = positions.shape[0]
    accumulated = jnp.zeros((row_count,) + extended.shape[1:], jnp.float32)
    for shift_by in range(tap_count):
        tap_rows = extended[tap_count - 1 - shift_by : tap_count - 1 - shift_by + row_count].astype(
            jnp.float32
        )
        usable = (positions - shift_by >= first_token).reshape(
            (row_count,) + (1,) * (extended.ndim - 1)
        )
        accumulated = accumulated + jnp.where(
            usable, tap_rows * taps[tap_count - 1 - shift_by], 0.0
        )
    return accumulated


def combine_states(earlier, following):
    return (earlier[0] * following[0], earlier[1] * following[0][:, None, None] + following[1])


def on_device(
    queries,
    key_rows,
    value_rows,
    doc_lengths,
    gate_input,
    bc_input,
    step_size,
    decay_rate,
    skip_gain,
    conv_x,
    conv_bc,
    norm_gain,
):
    row_count = queries.shape[0]
    head_size = key_rows.shape[1]
    head_count = queries.shape[1] // head_size
    score_scale = 1.0 / math.sqrt(head_size)
    ctx_index = lax.axis_index("ctx")
    block_start = ctx_index * row_count
    own_pos = block_start + jnp.arange(row_count, dtype=jnp.int32)
    own_first = first_positions(doc_lengths, own_pos)
    initial = (
        jnp.full((head_count, row_count), NEGATIVE_FILL, jnp.float32),
        jnp.zeros((head_count, row_count), jnp.float32),
        jnp.zeros((head_count, row_count, head_size), jnp.float32),
    )
    query_rows = queries.reshape(row_count, head_count, head_size)
    running = key_folder(query_rows, own_pos, own_first, score_scale)(
        initial,
        (
            lax.all_gather(key_rows, "ctx", axis=0, tiled=True),
            lax.all_gather(value_rows, "ctx", axis=0, tiled=True),
        ),
        jnp.int32(0),
    )
    attended = finish(running, row_count)
    group_index = lax.axis_index("tp") // 2
    bc_local = lax.dynamic_index_in_dim(bc_input, group_index, 2, keepdims=False)
    conv_bc_local = lax.dynamic_index_in_dim(conv_bc, group_index, 2, keepdims=False)
    tap_count = conv_x.shape[0]
    rim_input, rim_bc = from_behind(
        (attended[row_count - tap_count + 1 :], bc_local[row_count - tap_count + 1 :]), "ctx", 1
    )
    mixed_input = jax.nn.silu(
        causal_local(
            jnp.concatenate([rim_input, attended], 0), conv_x, own_pos, own_first, tap_count
        )
    ).astype(jnp.bfloat16)
    bc_conv = jax.nn.silu(
        causal_local(
            jnp.concatenate([rim_bc, bc_local], 0), conv_bc_local, own_pos, own_first, tap_count
        )
    ).astype(jnp.bfloat16)
    heads_local = step_size.shape[1]
    input_heads = mixed_input.reshape(row_count, heads_local, -1)
    b_values = bc_conv[:, 0]
    c_values = bc_conv[:, 1]
    highest = lax.Precision.HIGHEST
    log_decay = -decay_rate[None, :] * step_size
    cumulated = jnp.cumsum(log_decay, axis=0)
    gram_matrix = jnp.dot(c_values, b_values.T, preferred_element_type=jnp.float32)
    visible = (own_pos[None, :] >= own_first[:, None]) & (own_pos[None, :] <= own_pos[:, None])
    cum_heads = cumulated.T
    log_gap = jnp.where(visible[None], cum_heads[:, :, None] - cum_heads[:, None, :], -jnp.inf)
    mixing = gram_matrix[None] * jnp.exp(log_gap) * step_size.T[:, None, :]
    input_wide = input_heads.astype(jnp.float32)
    inner_part = jnp.einsum("hts,shp->thp", mixing, input_wide, precision=highest)
    last_start = own_first[-1]
    state_weight = jnp.where(
        (own_pos >= last_start)[:, None], jnp.exp(cumulated[-1][None, :] - cumulated), 0.0
    )
    state_weight = state_weight * step_size
    block_state = jnp.einsum(
        "shp,sn->hpn",
        state_weight[:, :, None] * input_wide,
        b_values.astype(jnp.float32),
        precision=highest,
    )
    carry_decay = jnp.where(last_start < block_start, jnp.exp(cumulated[-1]), 0.0)
    identity = (jnp.ones_like(carry_decay), jnp.zeros_like(block_state))
    _, incoming = prefix((carry_decay, block_state), "ctx", combine_states, identity)
    carry_in = (own_first < block_start).astype(jnp.float32)
    carried_part = jnp.einsum(
        "tn,hpn->thp", c_values.astype(jnp.float32), incoming, precision=highest
    )
    carried_part = carried_part * (jnp.exp(cumulated) * carry_in[:, None])[:, :, None]
    ssm_out = inner_part + carried_part + skip_gain[None, :, None] * input_wide
    gated = ssm_out.reshape(row_count, -1) * jax.nn.silu(gate_input.astype(jnp.float32))
    square_sum = jnp.sum(gated * gated, axis=1)
    partner_sum = swapped(square_sum, "tp", 0)
    mean_square = (square_sum + partner_sum) / (2 * gated.shape[1])
    return (gated * lax.rsqrt(mean_square + EPSILON)[:, None] * norm_gain[None, :]).astype(
        jnp.bfloat16
    )


LANES = 128
RIM = 16
MESH = pl.DeviceIdType.MESH


def dot_nt(a, b):
    return lax.dot_general(a, b, (((1,), (1,)), ((), ())), preferred_element_type=jnp.float32)


def dot_tn(a, b):
    return lax.dot_general(a, b, (((0,), (0,)), ((), ())), preferred_element_type=jnp.float32)


def dot_nn(a, b):
    return jnp.dot(a, b, preferred_element_type=jnp.float32)


def silu(v):
    return v / (1.0 + jnp.exp(-v))


def fused_kernel(
    n,
    window,
    doc_ref,
    rate_ref,
    skip_ref,
    q_in,
    k_in,
    v_in,
    gate_in,
    bc_in,
    step_in,
    taps_in,
    bc_taps_in,
    gain_in,
    out_ref,
    q_ref,
    gate_ref,
    bc_ref,
    step_ref,
    taps_ref,
    bc_taps_ref,
    gain_ref,
    load_sem,
    kv,
    q_rim,
    bc_rim,
    bc_all,
    x_out,
    x_all,
    dt_own,
    dt_all,
    mix_ref,
    weight_ref,
    carry_ref,
    state_ref,
    y_out,
    y_all,
    gated_ref,
    sq_own,
    sq_other,
    kv_send,
    kv_recv,
    rim_send,
    rim_recv,
    bc_send,
    bc_pass,
    bc_recv,
    bc_core_send,
    bc_core_recv,
    x_send,
    x_recv,
    dt_send,
    dt_recv,
    y_send,
    y_recv,
    sq_sem,
):
    loads = [
        pltpu.make_async_copy(src, dst, load_sem.at[i])
        for i, (src, dst) in enumerate((
            (k_in, kv.at[0, 0]), (v_in, kv.at[0, 1]), (bc_in, bc_ref), (q_in, q_ref),
            (step_in, step_ref), (bc_taps_in, bc_taps_ref), (taps_in, taps_ref),
            (gate_in, gate_ref), (gain_in, gain_ref)))
    ]
    for load in loads:
        load.start()
    rows = q_ref.shape[0]
    me = lax.axis_index("ctx")
    tp = lax.axis_index("tp")
    core = lax.rem(tp, 2)
    group = tp // 2
    tp_other = tp + 1 - 2 * core
    parity = lax.rem(me, 2)
    pair = me + 1 - 2 * parity
    state_size = bc_all.shape[3]
    ndoc = doc_ref.shape[0]
    groups = bc_ref.shape[1] // (2 * state_size)

    def to_ctx(src, dst, send, recv, where):
        return pltpu.make_async_remote_copy(
            src_ref=src, dst_ref=dst, send_sem=send, recv_sem=recv,
            device_id=(where, tp), device_id_type=MESH)

    def to_core(src, dst, send, recv):
        return pltpu.make_async_remote_copy(
            src_ref=src, dst_ref=dst, send_sem=send, recv_sem=recv,
            device_id=(me, tp_other), device_id_type=MESH)

    barrier = pltpu.get_barrier_semaphore()
    for k in range(1, n):
        pl.semaphore_signal(
            barrier, inc=1, device_id=(lax.rem(me + k, n), tp), device_id_type=MESH)
    pl.semaphore_signal(barrier, inc=1, device_id=(me, tp_other), device_id_type=MESH)
    for r in range(1, window):
        @pl.when(me < r)
        def _():
            kv[r] = jnp.zeros(kv.shape[1:], kv.dtype)

    @pl.when(me == 0)
    def _():
        q_rim[...] = jnp.zeros(q_rim.shape, q_rim.dtype)
        bc_rim[...] = jnp.zeros(bc_rim.shape, bc_rim.dtype)

    for load in loads:
        load.wait()
    steps = step_ref[...]
    for d in range(n):
        dt_own[d, 0:2] = steps[2 * d:2 * d + 2]

    pl.semaphore_wait(barrier, n)

    half = window // 2
    direct = []
    for k in range(1, half + 1):
        copy = to_ctx(kv.at[2 * k - 2], kv.at[2 * k], kv_send.at[k], kv_recv.at[2 * k],
                      jnp.minimum(me + 2, n - 1))
        wanted = (me + 2 < n) & (me >= 2 * k - 2)
        if 2 * k >= window:
            wanted = wanted & (parity == 1)
        direct.append((wanted, copy))
    even = parity == 0
    odd = parity == 1
    relay_even = [to_ctx(kv.at[r], kv.at[r + 1], kv_send.at[half + 1 + r], kv_recv.at[r + 1], pair)
                  for r in range(0, window, 2)]
    relay_odd = [to_ctx(kv.at[r], kv.at[r - 1], kv_send.at[half + 1 + r], kv_recv.at[r - 1], pair)
                 for r in range(2, window + 1, 2)]
    nxt = jnp.minimum(me + 1, n - 1)
    rim_q = to_ctx(q_ref.at[pl.ds(rows - RIM, RIM)], q_rim, rim_send.at[0], rim_recv.at[0], nxt)
    rim_b = to_ctx(bc_ref.at[pl.ds(rows - RIM, RIM)], bc_rim, rim_send.at[1], rim_recv.at[1], nxt)

    @pl.when(me + 1 < n)
    def _():
        rim_b.start()

    @pl.when(even)
    def _():
        relay_even[0].start()

    @pl.when(direct[0][0])
    def _():
        direct[0][1].start()

    @pl.when(me + 1 < n)
    def _():
        rim_q.start()

    for k in range(1, n):
        d = lax.rem(me + k, n)
        to_ctx(dt_own.at[d], dt_all.at[me], dt_send.at[k], dt_recv.at[me], d).start()
    dt_all[me] = dt_own[me]

    starts = []
    total = jnp.int32(0)
    for i in range(ndoc):
        starts.append(total)
        total = total + doc_ref[i]

    def first_of(pos):
        first = jnp.zeros_like(pos)
        for s in starts:
            first = jnp.where(s <= pos, s, first)
        return first

    row_iota = lax.broadcasted_iota(jnp.int32, (rows, LANES), 0)
    lane_iota = lax.broadcasted_iota(jnp.int32, (rows, LANES), 1)
    base = me * rows
    own_pos = base + row_iota
    own_first = first_of(own_pos)
    tap_count = taps_ref.shape[0]
    since = own_pos - own_first

    def conv(extended, taps):
        acc = None
        for m in range(tap_count):
            part = extended[8 - m: 8 - m + rows] * taps[tap_count - 1 - m: tap_count - m]
            part = jnp.where(since >= m, part, 0.0)
            acc = part if acc is None else acc + part
        return silu(acc).astype(jnp.bfloat16)

    @pl.when(me > 0)
    def _():
        rim_b.wait_recv()

    for i in range(2):
        for piece in range(state_size // LANES):
            cols = pl.ds(pl.multiple_of(
                (i * groups + group) * state_size + piece * LANES, LANES), LANES)
            extended = jnp.concatenate(
                [bc_rim[:, cols].astype(jnp.float32)[RIM - 8:], bc_ref[:, cols].astype(jnp.float32)], axis=0)
            lanes = slice(piece * LANES, (piece + 1) * LANES)
            taps = jnp.zeros((tap_count, LANES), jnp.float32)
            for g in range(groups):
                part = jnp.concatenate(
                    [bc_taps_ref[m, i, g:g + 1, lanes] for m in range(tap_count)], axis=0)
                taps = jnp.where(group == g, part, taps)
            bc_all[me, i, :, piece * LANES:(piece + 1) * LANES] = conv(extended, taps)

    def bc_copy(s, sem, where):
        return to_ctx(bc_all.at[s, core], bc_all.at[s, core], sem, bc_recv.at[s], where)

    def share_bc(s):
        return to_core(bc_all.at[s, core], bc_all.at[s, core], bc_core_send.at[s], bc_core_recv.at[s])

    has_up, has_down = me + 2 < n, me >= 2
    above, below = jnp.minimum(me + 2, n - 1), jnp.maximum(me - 2, 0)
    bc_pair = bc_copy(me, bc_send.at[me], pair)
    bc_up = bc_copy(me, bc_pass.at[me], above)
    bc_down = bc_copy(me, bc_pass.at[n], below)
    column = []
    for k in range(1, n // 2):
        column.append((me >= 2 * k, jnp.maximum(me - 2 * k, 0), has_up, above))
        column.append((me + 2 * k < n, jnp.minimum(me + 2 * k, n - 1), has_down, below))

    for r in range(2, window + 1, 2):
        cond = me >= r
        if r >= window:
            cond = cond & odd

        @pl.when(cond)
        def _():
            to_ctx(kv.at[0], kv.at[r], kv_send.at[0], kv_recv.at[r], pair).wait_recv()

        if r // 2 < len(direct):
            @pl.when(direct[r // 2][0])
            def _():
                direct[r // 2][1].start()
        if r == 2:
            bc_pair.start()

            @pl.when(has_up)
            def _():
                bc_up.start()

            @pl.when(has_down)
            def _():
                bc_down.start()
        if r < window:
            @pl.when(even & (me >= r))
            def _():
                relay_even[r // 2].start()

        @pl.when(odd & (me >= r))
        def _():
            relay_odd[r // 2 - 1].start()
    for r in range(1, window, 2):
        @pl.when(me >= r)
        def _():
            to_ctx(kv.at[0], kv.at[r], kv_send.at[0], kv_recv.at[r], pair).wait_recv()

    @pl.when(me > 0)
    def _():
        rim_q.wait_recv()

    keys = jnp.concatenate([kv[r, 0] for r in range(window)], axis=0)
    values = jnp.concatenate([kv[r, 1] for r in range(window)], axis=0)
    values = jnp.concatenate([values, jnp.ones_like(values)], axis=1)
    scale = math.log2(math.e) / math.sqrt(k_in.shape[1])

    def bias_of(pos):
        first = first_of(pos)
        parts = []
        for r in range(window):
            key_pos = (me - r) * rows + lane_iota
            parts.append(jnp.where((key_pos <= pos) & (key_pos >= first), 0.0, NEGATIVE_FILL))
        return jnp.concatenate(parts, axis=1)

    def attention(block, bias):
        scores = dot_nt(block, keys) + bias
        exponent = jnp.exp2((scores - jnp.max(scores, axis=1, keepdims=True)) * scale)
        summed = dot_nn(exponent.astype(jnp.bfloat16), values)
        return (summed[:, :LANES] / summed[:, LANES:]).astype(jnp.bfloat16).astype(jnp.float32)

    rim_block = jnp.concatenate(
        [q_rim[:, h * LANES:(h + 1) * LANES] for h in range(n)], axis=0)
    rim_pos = base - RIM + lax.rem(row_iota, RIM)
    gated_ref[0] = attention(rim_block, bias_of(rim_pos))
    bias = bias_of(own_pos)

    def recv_bc(s):
        to_ctx(bc_all.at[s, core], bc_all.at[s, core], bc_send.at[0], bc_recv.at[s], pair).wait_recv()

    crossed = [pair] + [lax.rem(pair + 2 * k, n) for k in range(1, n // 2)]
    for k in range(n):
        h = lax.rem(me + 1 + k, n)
        cols = pl.ds(pl.multiple_of(h * LANES, LANES), LANES)
        attended = attention(q_ref[:, cols], bias)
        rim = gated_ref[0, pl.ds(pl.multiple_of(h * RIM + RIM - 8, 8), 8), :]
        x = conv(jnp.concatenate([rim, attended], axis=0), taps_ref[:, cols])
        if k < n - 1:
            x_out[h] = x
            to_ctx(x_out.at[h], x_all.at[me], x_send.at[k], x_recv.at[me], h).start()
        else:
            x_all[me] = x
        if 1 <= k < n // 2:
            for here, s, onward, where in column[2 * k - 2:2 * k]:
                @pl.when(here)
                def _():
                    recv_bc(s)

                    @pl.when(onward)
                    def _():
                        bc_copy(s, bc_pass.at[s], where).start()

                    bc_copy(s, bc_send.at[s], pair).start()
                    share_bc(s).start()
        if n // 2 <= k:
            s = crossed[k - n // 2]
            recv_bc(s)
            share_bc(s).start()

    upper = (row_iota <= lane_iota).astype(jnp.float32)
    left = lane_iota < LANES // 2
    rate = [rate_ref[2 * me + a] for a in range(2)]
    skip = jnp.where(left[:1], skip_ref[2 * me], skip_ref[2 * me + 1])
    for k in range(1, n):
        s = lax.rem(me + k, n)
        to_ctx(dt_own.at[s], dt_all.at[s], dt_send.at[k], dt_recv.at[s], s).wait_recv()
    dt_rows = [jnp.concatenate([dt_all[i, a:a + 1] for i in range(n)], axis=0) for a in range(2)]
    cum_rows = [jnp.dot(-rate[a] * dt_rows[a], upper, precision=lax.Precision.HIGHEST,
                        preferred_element_type=jnp.float32) for a in range(2)]
    keeps = []
    other = 1 - core
    for k in range(1, n):
        s = lax.rem(me + k, n)
        to_core(bc_all.at[s, other], bc_all.at[s, other], bc_core_send.at[0],
                bc_core_recv.at[s]).wait_recv()
    for i in range(n):
        start = i * rows
        pos = start + row_iota
        first = first_of(pos)
        key_pos = start + lane_iota
        visible = (key_pos >= first) & (key_pos <= pos)
        cum = [cum_rows[a][i:i + 1] for a in range(2)]
        dts = [dt_rows[a][i:i + 1] for a in range(2)]
        side = (rows // 2, LANES)
        cum_col = jnp.concatenate([jnp.broadcast_to(r, side) for r in cum], axis=0).T
        dt_col = jnp.concatenate([jnp.broadcast_to(r, side) for r in dts], axis=0).T
        gram = jnp.where(visible, dot_nt(bc_all[i, 1], bc_all[i, 0]), 0.0)
        for a in range(2):
            col = cum_col[:, a * (LANES // 2):a * (LANES // 2) + 1]
            gap = jnp.where(visible, col - cum[a], 0.0)
            mix_ref[i, :, a * LANES:(a + 1) * LANES] = (
                gram * jnp.exp(gap) * dts[a]).astype(jnp.bfloat16)
        last_start = first[rows - 1:rows]
        cum_last = cum_col[rows - 1:rows]
        carry_ref[i] = jnp.where(first < start, jnp.exp(cum_col), 0.0)
        weight_ref[i] = jnp.where(pos >= last_start, jnp.exp(cum_last - cum_col) * dt_col, 0.0)
        keeps.append(jnp.where(last_start < start, jnp.exp(cum_last), 0.0))

    state = jnp.zeros((state_size, LANES), jnp.float32)
    for k in range(1, n):
        s = lax.rem(me + n - k, n)
        to_ctx(x_all.at[s], x_all.at[s], x_send.at[0], x_recv.at[s], pair).wait_recv()
    for i in range(n):
        state_ref[i] = state.astype(jnp.bfloat16)
        if i < n - 1:
            weighted = (x_all[i].astype(jnp.float32) * weight_ref[i]).astype(jnp.bfloat16)
            state = keeps[i] * state + dot_tn(bc_all[i, 0], weighted)

    for k in range(n):
        i = lax.rem(me + 1 + k, n)
        xw = x_all[i].astype(jnp.float32)
        both = jnp.concatenate([jnp.where(left, xw, 0.0), jnp.where(left, 0.0, xw)], axis=0)
        y = dot_nn(mix_ref[i], both.astype(jnp.bfloat16)) + skip * xw
        y = (y + carry_ref[i] * dot_nn(bc_all[i, 1], state_ref[i])).astype(jnp.bfloat16)
        if k < n - 1:
            y_out[i] = y
            to_ctx(y_out.at[i], y_all.at[me], y_send.at[i], y_recv.at[me], i).start()
        else:
            y_all[me] = y

    squares = jnp.zeros((rows, LANES), jnp.float32)
    for k in range(n):
        h = lax.rem(me + n - 1 - k, n)
        if k < n - 1:
            to_ctx(y_out.at[h], y_all.at[h], y_send.at[h], y_recv.at[h], h).wait_recv()
        z = gate_ref[:, pl.ds(pl.multiple_of(h * LANES, LANES), LANES)].astype(jnp.float32)
        gated = y_all[h].astype(jnp.float32) * silu(z)
        gated_ref[h] = gated
        squares = squares + gated * gated
    sq_own[...] = squares
    swap = to_core(sq_own, sq_other, sq_sem.at[0], sq_sem.at[1])
    swap.start()

    for wanted, copy in direct:
        @pl.when(wanted)
        def _():
            copy.wait_send()
    for j, r in enumerate(range(0, window, 2)):
        @pl.when(even & (me >= r))
        def _():
            relay_even[j].wait_send()
    for j, r in enumerate(range(2, window + 1, 2)):
        @pl.when(odd & (me >= r))
        def _():
            relay_odd[j].wait_send()

    @pl.when(me + 1 < n)
    def _():
        rim_q.wait_send()
        rim_b.wait_send()
    bc_pair.wait_send()

    @pl.when(has_up)
    def _():
        bc_up.wait_send()

    @pl.when(has_down)
    def _():
        bc_down.wait_send()
    for here, s, onward, where in column:
        @pl.when(here)
        def _():
            bc_copy(s, bc_send.at[s], pair).wait_send()
            share_bc(s).wait_send()

            @pl.when(onward)
            def _():
                bc_copy(s, bc_pass.at[s], where).wait_send()
    for s in crossed:
        share_bc(s).wait_send()
    for k in range(n - 1):
        h = lax.rem(me + 1 + k, n)
        to_ctx(x_out.at[h], x_all.at[me], x_send.at[k], x_recv.at[me], h).wait_send()
        to_ctx(dt_own.at[h], dt_all.at[me], dt_send.at[k + 1], dt_recv.at[me], h).wait_send()
    for i in range(n):
        @pl.when(me != i)
        def _():
            to_ctx(y_out.at[i], y_all.at[me], y_send.at[i], y_recv.at[me], i).wait_send()
    swap.wait()
    width = 2 * n * LANES
    mean_square = jnp.sum(sq_own[...] + sq_other[...], axis=1, keepdims=True) / width
    factor = lax.rsqrt(mean_square + EPSILON)
    for h in range(n):
        cols = slice(h * LANES, (h + 1) * LANES)
        out_ref[:, cols] = (gated_ref[h] * factor * gain_ref[:, cols]).astype(jnp.bfloat16)


def fused_on_device(
    queries, key_rows, value_rows, doc_lengths, gate_input, bc_input, step_size,
    decay_rate, skip_gain, conv_x, conv_bc, norm_gain,
):
    n = lax.axis_size("ctx")
    rows = queries.shape[0]
    state_size = bc_input.shape[3]
    longest = n * rows // 2 + 64
    window = 1 + -(-(longest - 1) // rows)
    bc = bc_input.reshape(rows, -1)
    bf16, f32 = jnp.bfloat16, jnp.float32
    hbm = pl.BlockSpec(memory_space=pl.ANY)
    vmem = pl.BlockSpec(memory_space=pltpu.VMEM)
    smem = pl.BlockSpec(memory_space=pltpu.SMEM)
    dma = pltpu.SemaphoreType.DMA
    half = window // 2
    return pl.pallas_call(
        functools.partial(fused_kernel, n, window),
        out_shape=jax.ShapeDtypeStruct(queries.shape, bf16),
        in_specs=[smem] * 3 + [hbm] * 9,
        out_specs=vmem,
        scratch_shapes=[
            pltpu.VMEM(queries.shape, bf16),
            pltpu.VMEM(gate_input.shape, bf16),
            pltpu.VMEM(bc.shape, bf16),
            pltpu.VMEM(step_size.shape[::-1], f32),
            pltpu.VMEM(conv_x.shape, f32),
            pltpu.VMEM(conv_bc.shape, f32),
            pltpu.VMEM((1, norm_gain.shape[0]), f32),
            dma((9,)),
            pltpu.VMEM((window + 1, 2, rows, LANES), bf16),
            pltpu.VMEM((RIM, queries.shape[1]), bf16),
            pltpu.VMEM((RIM, bc.shape[1]), bf16),
            pltpu.VMEM((n, 2, rows, state_size), bf16),
            pltpu.VMEM((n, rows, LANES), bf16),
            pltpu.VMEM((n, rows, LANES), bf16),
            pltpu.VMEM((n, 8, LANES), f32),
            pltpu.VMEM((n, 8, LANES), f32),
            pltpu.VMEM((n, rows, 2 * LANES), bf16),
            pltpu.VMEM((n, rows, LANES), f32),
            pltpu.VMEM((n, rows, LANES), f32),
            pltpu.VMEM((n, state_size, LANES), bf16),
            pltpu.VMEM((n, rows, LANES), bf16),
            pltpu.VMEM((n, rows, LANES), bf16),
            pltpu.VMEM((n, rows, LANES), f32),
            pltpu.VMEM((rows, LANES), f32),
            pltpu.VMEM((rows, LANES), f32),
            dma((half + 2 + window,)),
            dma((window + 1,)),
            dma((2,)),
            dma((2,)),
            dma((n,)),
            dma((n + 1,)),
            dma((n,)),
            dma((n,)),
            dma((n,)),
            dma((n,)),
            dma((n,)),
            dma((n,)),
            dma((n,)),
            dma((n,)),
            dma((n,)),
            dma((2,)),
        ],
        compiler_params=pltpu.CompilerParams(
            collective_id=0, has_side_effects=True, vmem_limit_bytes=58 * 1024 * 1024),
    )(
        doc_lengths, decay_rate, skip_gain, queries, key_rows, value_rows, gate_input, bc, step_size.T,
        conv_x, conv_bc, norm_gain.reshape(1, -1),
    )


def plan(queries, key_rows, *rest):
    blocks = queries.shape[1] // LANES
    if blocks == lax.axis_size("ctx") and queries.shape[0] == LANES:
        return fused_on_device(queries, key_rows, *rest)
    return on_device(queries, key_rows, *rest)


def solution(mesh):
    return jax.shard_map(
        plan,
        mesh=mesh,
        in_specs=(
            P("ctx", "tp"),
            P("ctx", "tp"),
            P("ctx", "tp"),
            P(),
            P("ctx", "tp"),
            P("ctx", None, None, None),
            P("ctx", "tp"),
            P("tp"),
            P("tp"),
            P(None, "tp"),
            P(),
            P("tp"),
        ),
        out_specs=P("ctx", "tp"),
        check_vma=False,
    )
```

```python
import functools
import math

import jax
import jax.numpy as jnp
from jax import lax
from jax.experimental import pallas as pl
from jax.experimental.pallas import tpu as pltpu
from jax.sharding import PartitionSpec as P

EPSILON = 1e-05
NEGATIVE_FILL = -1e30


def from_behind(x, axis, by):
    size = lax.axis_size(axis)
    pairs = [(i, i + by) for i in range(size) if 0 <= i + by < size]
    return lax.ppermute(x, axis, pairs)


def prefix(x, axis, combine, identity):
    size, mine = (lax.axis_size(axis), lax.axis_index(axis))
    everything = jax.tree.map(
        lambda part, kind: lax.all_gather(part.astype(kind), axis), x, (jnp.bfloat16, jnp.bfloat16)
    )
    start = jax.tree.map(
        lambda part, zero: jnp.broadcast_to(jnp.asarray(zero, part.dtype), part.shape), x, identity
    )

    def step(k, before):
        reached = k < mine
        new = combine(
            before, jax.tree.map(lambda part, own: part[k].astype(own.dtype), everything, x)
        )
        return jax.tree.map(lambda a, b: jnp.where(reached, a, b), new, before)

    return lax.fori_loop(0, size, step, start)


def swapped(block, axis, bit):
    count = lax.axis_size(axis)
    route = []
    for low in range(count):
        high = low | 1 << bit
        if high != low and high < count:
            route += [(low, high), (high, low)]
    return lax.ppermute(block, axis, route)


def first_positions(doc_lengths, positions):
    doc_ends = jnp.cumsum(doc_lengths)
    doc_starts = doc_ends - doc_lengths
    covered = doc_starts[None, :] <= positions[:, None]
    return jnp.max(
        jnp.where(covered, doc_starts[None, :], jnp.zeros_like(doc_starts)[None, :]), axis=1
    )


def attend(
    running, key_block, value_block, key_start, query_rows, query_pos, query_first, score_scale
):
    maximum, totals, summed = running
    key_pos = key_start + jnp.arange(key_block.shape[0], dtype=jnp.int32)
    scores = (
        jnp.einsum("qhd,kd->hqk", query_rows, key_block, preferred_element_type=jnp.float32)
        * score_scale
    )
    visible = (
        (key_pos[None, :] <= query_pos[:, None]) & (key_pos[None, :] >= query_first[:, None])
    )[None]
    masked = jnp.where(visible, scores, NEGATIVE_FILL)
    new_maximum = jnp.maximum(maximum, jnp.max(masked, axis=-1))
    exponent = jnp.where(visible, jnp.exp(masked - new_maximum[..., None]), 0.0)
    factor = jnp.exp(maximum - new_maximum)
    totals = totals * factor + jnp.sum(exponent, axis=-1)
    weights = exponent.astype(jnp.bfloat16)
    summed = summed * factor[..., None] + jnp.einsum(
        "hqk,kd->hqd", weights, value_block, preferred_element_type=jnp.float32
    )
    return (new_maximum, totals, summed)


def key_folder(query_rows, query_pos, query_first, score_scale):
    query_last = jnp.max(query_pos)
    earliest = jnp.min(query_first)

    def maybe_attend(running, key_slab, value_slab, key_start):
        needed = (key_start <= query_last) & (key_start + key_slab.shape[0] > earliest)

        def compute(inner_run):
            return attend(
                inner_run,
                key_slab,
                value_slab,
                key_start,
                query_rows,
                query_pos,
                query_first,
                score_scale,
            )

        def keep(inner_run):
            return inner_run

        return lax.cond(needed, compute, keep, running)

    def fold_keys(running, pieces, offset):
        key_block, value_block = pieces
        key_count = key_block.shape[0]
        block_width = 256
        block_count = key_count // block_width

        def visit(inner_run, entries):
            block_index, key_slab, value_slab = entries
            return (maybe_attend(inner_run, key_slab, value_slab, block_index * block_width), None)

        running, _ = lax.scan(
            visit,
            running,
            (
                jnp.arange(block_count, dtype=jnp.int32),
                key_block.reshape(block_count, block_width, -1),
                value_block.reshape(block_count, block_width, -1),
            ),
        )
        return running

    return fold_keys


def finish(running, row_count):
    maximum, totals, summed = running
    output = summed / totals[..., None]
    return jnp.transpose(output, (1, 0, 2)).reshape(row_count, -1).astype(jnp.bfloat16)


def causal_local(extended, taps, positions, first_token, tap_count):
    row_count = positions.shape[0]
    accumulated = jnp.zeros((row_count,) + extended.shape[1:], jnp.float32)
    for shift_by in range(tap_count):
        tap_rows = extended[tap_count - 1 - shift_by : tap_count - 1 - shift_by + row_count].astype(
            jnp.float32
        )
        usable = (positions - shift_by >= first_token).reshape(
            (row_count,) + (1,) * (extended.ndim - 1)
        )
        accumulated = accumulated + jnp.where(
            usable, tap_rows * taps[tap_count - 1 - shift_by], 0.0
        )
    return accumulated


def combine_states(earlier, following):
    return (earlier[0] * following[0], earlier[1] * following[0][:, None, None] + following[1])


def on_device(
    queries,
    key_rows,
    value_rows,
    doc_lengths,
    gate_input,
    bc_input,
    step_size,
    decay_rate,
    skip_gain,
    conv_x,
    conv_bc,
    norm_gain,
):
    row_count = queries.shape[0]
    head_size = key_rows.shape[1]
    head_count = queries.shape[1] // head_size
    score_scale = 1.0 / math.sqrt(head_size)
    ctx_index = lax.axis_index("ctx")
    block_start = ctx_index * row_count
    own_pos = block_start + jnp.arange(row_count, dtype=jnp.int32)
    own_first = first_positions(doc_lengths, own_pos)
    initial = (
        jnp.full((head_count, row_count), NEGATIVE_FILL, jnp.float32),
        jnp.zeros((head_count, row_count), jnp.float32),
        jnp.zeros((head_count, row_count, head_size), jnp.float32),
    )
    query_rows = queries.reshape(row_count, head_count, head_size)
    running = key_folder(query_rows, own_pos, own_first, score_scale)(
        initial,
        (
            lax.all_gather(key_rows, "ctx", axis=0, tiled=True),
            lax.all_gather(value_rows, "ctx", axis=0, tiled=True),
        ),
        jnp.int32(0),
    )
    attended = finish(running, row_count)
    group_index = lax.axis_index("tp") // 2
    bc_local = lax.dynamic_index_in_dim(bc_input, group_index, 2, keepdims=False)
    conv_bc_local = lax.dynamic_index_in_dim(conv_bc, group_index, 2, keepdims=False)
    tap_count = conv_x.shape[0]
    rim_input, rim_bc = from_behind(
        (attended[row_count - tap_count + 1 :], bc_local[row_count - tap_count + 1 :]), "ctx", 1
    )
    mixed_input = jax.nn.silu(
        causal_local(
            jnp.concatenate([rim_input, attended], 0), conv_x, own_pos, own_first, tap_count
        )
    ).astype(jnp.bfloat16)
    bc_conv = jax.nn.silu(
        causal_local(
            jnp.concatenate([rim_bc, bc_local], 0), conv_bc_local, own_pos, own_first, tap_count
        )
    ).astype(jnp.bfloat16)
    heads_local = step_size.shape[1]
    input_heads = mixed_input.reshape(row_count, heads_local, -1)
    b_values = bc_conv[:, 0]
    c_values = bc_conv[:, 1]
    highest = lax.Precision.HIGHEST
    log_decay = -decay_rate[None, :] * step_size
    cumulated = jnp.cumsum(log_decay, axis=0)
    gram_matrix = jnp.dot(c_values, b_values.T, preferred_element_type=jnp.float32)
    visible = (own_pos[None, :] >= own_first[:, None]) & (own_pos[None, :] <= own_pos[:, None])
    cum_heads = cumulated.T
    log_gap = jnp.where(visible[None], cum_heads[:, :, None] - cum_heads[:, None, :], -jnp.inf)
    mixing = gram_matrix[None] * jnp.exp(log_gap) * step_size.T[:, None, :]
    input_wide = input_heads.astype(jnp.float32)
    inner_part = jnp.einsum("hts,shp->thp", mixing, input_wide, precision=highest)
    last_start = own_first[-1]
    state_weight = jnp.where(
        (own_pos >= last_start)[:, None], jnp.exp(cumulated[-1][None, :] - cumulated), 0.0
    )
    state_weight = state_weight * step_size
    block_state = jnp.einsum(
        "shp,sn->hpn",
        state_weight[:, :, None] * input_wide,
        b_values.astype(jnp.float32),
        precision=highest,
    )
    carry_decay = jnp.where(last_start < block_start, jnp.exp(cumulated[-1]), 0.0)
    identity = (jnp.ones_like(carry_decay), jnp.zeros_like(block_state))
    _, incoming = prefix((carry_decay, block_state), "ctx", combine_states, identity)
    carry_in = (own_first < block_start).astype(jnp.float32)
    carried_part = jnp.einsum(
        "tn,hpn->thp", c_values.astype(jnp.float32), incoming, precision=highest
    )
    carried_part = carried_part * (jnp.exp(cumulated) * carry_in[:, None])[:, :, None]
    ssm_out = inner_part + carried_part + skip_gain[None, :, None] * input_wide
    gated = ssm_out.reshape(row_count, -1) * jax.nn.silu(gate_input.astype(jnp.float32))
    square_sum = jnp.sum(gated * gated, axis=1)
    partner_sum = swapped(square_sum, "tp", 0)
    mean_square = (square_sum + partner_sum) / (2 * gated.shape[1])
    return (gated * lax.rsqrt(mean_square + EPSILON)[:, None] * norm_gain[None, :]).astype(
        jnp.bfloat16
    )


LANES = 128
RIM = 16
MESH = pl.DeviceIdType.MESH


def dot_nt(a, b):
    return lax.dot_general(a, b, (((1,), (1,)), ((), ())), preferred_element_type=jnp.float32)


def dot_tn(a, b):
    return lax.dot_general(a, b, (((0,), (0,)), ((), ())), preferred_element_type=jnp.float32)


def dot_nn(a, b):
    return jnp.dot(a, b, preferred_element_type=jnp.float32)


def silu(v):
    return v / (1.0 + jnp.exp(-v))


def fused_kernel(
    n,
    window,
    doc_ref,
    rate_ref,
    skip_ref,
    q_in,
    k_in,
    v_in,
    gate_in,
    bc_in,
    step_in,
    taps_in,
    bc_taps_in,
    gain_in,
    out_ref,
    q_ref,
    gate_ref,
    bc_ref,
    step_ref,
    taps_ref,
    bc_taps_ref,
    gain_ref,
    load_sem,
    kv,
    q_rim,
    bc_rim,
    bc_all,
    x_out,
    x_all,
    dt_own,
    dt_all,
    mix_ref,
    weight_ref,
    carry_ref,
    state_ref,
    y_out,
    y_all,
    gated_ref,
    sq_own,
    sq_other,
    kv_send,
    kv_recv,
    rim_send,
    rim_recv,
    bc_send,
    bc_recv,
    bc_core_send,
    bc_core_recv,
    x_send,
    x_recv,
    dt_send,
    dt_recv,
    y_send,
    y_recv,
    sq_sem,
):
    loads = [
        pltpu.make_async_copy(src, dst, load_sem.at[i])
        for i, (src, dst) in enumerate((
            (k_in, kv.at[0, 0]), (v_in, kv.at[0, 1]), (bc_in, bc_ref), (q_in, q_ref),
            (step_in, step_ref), (bc_taps_in, bc_taps_ref), (taps_in, taps_ref),
            (gate_in, gate_ref), (gain_in, gain_ref)))
    ]
    for load in loads:
        load.start()
    rows = q_ref.shape[0]
    me = lax.axis_index("ctx")
    tp = lax.axis_index("tp")
    core = lax.rem(tp, 2)
    group = tp // 2
    tp_other = tp + 1 - 2 * core
    parity = lax.rem(me, 2)
    pair = me + 1 - 2 * parity
    state_size = bc_all.shape[3]
    ndoc = doc_ref.shape[0]
    groups = bc_ref.shape[1] // (2 * state_size)

    def to_ctx(src, dst, send, recv, where):
        return pltpu.make_async_remote_copy(
            src_ref=src, dst_ref=dst, send_sem=send, recv_sem=recv,
            device_id=(where, tp), device_id_type=MESH)

    def to_core(src, dst, send, recv):
        return pltpu.make_async_remote_copy(
            src_ref=src, dst_ref=dst, send_sem=send, recv_sem=recv,
            device_id=(me, tp_other), device_id_type=MESH)

    barrier = pltpu.get_barrier_semaphore()
    for k in range(1, n):
        pl.semaphore_signal(
            barrier, inc=1, device_id=(lax.rem(me + k, n), tp), device_id_type=MESH)
    pl.semaphore_signal(barrier, inc=1, device_id=(me, tp_other), device_id_type=MESH)
    for r in range(1, window):
        @pl.when(me < r)
        def _():
            kv[r] = jnp.zeros(kv.shape[1:], kv.dtype)

    @pl.when(me == 0)
    def _():
        q_rim[...] = jnp.zeros(q_rim.shape, q_rim.dtype)
        bc_rim[...] = jnp.zeros(bc_rim.shape, bc_rim.dtype)

    for load in loads:
        load.wait()
    steps = step_ref[...]
    for d in range(n):
        dt_own[d, 0:2] = steps[2 * d:2 * d + 2]

    pl.semaphore_wait(barrier, n)

    half = window // 2
    direct = []
    for k in range(1, half + 1):
        copy = to_ctx(kv.at[0], kv.at[2 * k], kv_send.at[k], kv_recv.at[2 * k],
                      jnp.minimum(me + 2 * k, n - 1))
        wanted = me + 2 * k < n
        if 2 * k >= window:
            wanted = wanted & (parity == 1)
        direct.append((wanted, copy))
    even = parity == 0
    odd = parity == 1
    relay_even = [to_ctx(kv.at[r], kv.at[r + 1], kv_send.at[half + 1 + r], kv_recv.at[r + 1], pair)
                  for r in range(0, window, 2)]
    relay_odd = [to_ctx(kv.at[r], kv.at[r - 1], kv_send.at[half + 1 + r], kv_recv.at[r - 1], pair)
                 for r in range(2, window + 1, 2)]
    nxt = jnp.minimum(me + 1, n - 1)
    rim_q = to_ctx(q_ref.at[pl.ds(rows - RIM, RIM)], q_rim, rim_send.at[0], rim_recv.at[0], nxt)
    rim_b = to_ctx(bc_ref.at[pl.ds(rows - RIM, RIM)], bc_rim, rim_send.at[1], rim_recv.at[1], nxt)

    @pl.when(me + 1 < n)
    def _():
        rim_b.start()

    @pl.when(even)
    def _():
        relay_even[0].start()

    for wanted, copy in direct:
        @pl.when(wanted)
        def _():
            copy.start()

    @pl.when(me + 1 < n)
    def _():
        rim_q.start()

    for k in range(1, n):
        d = lax.rem(me + k, n)
        to_ctx(dt_own.at[d], dt_all.at[me], dt_send.at[k], dt_recv.at[me], d).start()
    dt_all[me] = dt_own[me]

    starts = []
    total = jnp.int32(0)
    for i in range(ndoc):
        starts.append(total)
        total = total + doc_ref[i]

    def first_of(pos):
        first = jnp.zeros_like(pos)
        for s in starts:
            first = jnp.where(s <= pos, s, first)
        return first

    row_iota = lax.broadcasted_iota(jnp.int32, (rows, LANES), 0)
    lane_iota = lax.broadcasted_iota(jnp.int32, (rows, LANES), 1)
    base = me * rows
    own_pos = base + row_iota
    own_first = first_of(own_pos)
    tap_count = taps_ref.shape[0]
    since = own_pos - own_first

    def conv(extended, taps):
        acc = None
        for m in range(tap_count):
            part = extended[8 - m: 8 - m + rows] * taps[tap_count - 1 - m: tap_count - m]
            part = jnp.where(since >= m, part, 0.0)
            acc = part if acc is None else acc + part
        return silu(acc).astype(jnp.bfloat16)

    @pl.when(me > 0)
    def _():
        rim_b.wait_recv()

    for i in range(2):
        for piece in range(state_size // LANES):
            cols = pl.ds(pl.multiple_of(
                (i * groups + group) * state_size + piece * LANES, LANES), LANES)
            extended = jnp.concatenate(
                [bc_rim[:, cols].astype(jnp.float32)[RIM - 8:], bc_ref[:, cols].astype(jnp.float32)], axis=0)
            lanes = slice(piece * LANES, (piece + 1) * LANES)
            taps = jnp.zeros((tap_count, LANES), jnp.float32)
            for g in range(groups):
                part = jnp.concatenate(
                    [bc_taps_ref[m, i, g:g + 1, lanes] for m in range(tap_count)], axis=0)
                taps = jnp.where(group == g, part, taps)
            bc_all[me, i, :, piece * LANES:(piece + 1) * LANES] = conv(extended, taps)

    column = [lax.rem(me + 2 * k, n) for k in range(1, n // 2)]

    def relay_bc(s, slot):
        return to_ctx(bc_all.at[s, core], bc_all.at[s, core], bc_send.at[slot], bc_recv.at[s], pair)

    def share_bc(s, slot):
        return to_core(bc_all.at[s, core], bc_all.at[s, core], bc_core_send.at[slot], bc_core_recv.at[s])

    bc_own = [to_ctx(bc_all.at[me, core], bc_all.at[me, core], bc_send.at[0], bc_recv.at[me], pair)]
    for k, d in enumerate(column):
        bc_own.append(to_ctx(bc_all.at[me, core], bc_all.at[me, core],
                             bc_send.at[1 + k], bc_recv.at[me], d))

    for r in range(2, window + 1, 2):
        cond = me >= r
        if r >= window:
            cond = cond & odd

        @pl.when(cond)
        def _():
            to_ctx(kv.at[0], kv.at[r], kv_send.at[0], kv_recv.at[r], pair).wait_recv()

        if r == 2:
            for copy in bc_own:
                copy.start()
        if r < window:
            @pl.when(even & (me >= r))
            def _():
                relay_even[r // 2].start()

        @pl.when(odd & (me >= r))
        def _():
            relay_odd[r // 2 - 1].start()
    for r in range(1, window, 2):
        @pl.when(me >= r)
        def _():
            to_ctx(kv.at[0], kv.at[r], kv_send.at[0], kv_recv.at[r], pair).wait_recv()

    @pl.when(me > 0)
    def _():
        rim_q.wait_recv()

    keys = jnp.concatenate([kv[r, 0] for r in range(window)], axis=0)
    values = jnp.concatenate([kv[r, 1] for r in range(window)], axis=0)
    values = jnp.concatenate([values, jnp.ones_like(values)], axis=1)
    scale = math.log2(math.e) / math.sqrt(k_in.shape[1])

    def bias_of(pos):
        first = first_of(pos)
        parts = []
        for r in range(window):
            key_pos = (me - r) * rows + lane_iota
            parts.append(jnp.where((key_pos <= pos) & (key_pos >= first), 0.0, NEGATIVE_FILL))
        return jnp.concatenate(parts, axis=1)

    def attention(blocks, biases):
        scores = dot_nt(jnp.concatenate(blocks, axis=0), keys)
        exponents = []
        for j, bias in enumerate(biases):
            part = scores[j * rows:(j + 1) * rows] + bias
            exponents.append(jnp.exp2(
                (part - jnp.max(part, axis=1, keepdims=True)) * scale).astype(jnp.bfloat16))
        summed = dot_nn(jnp.concatenate(exponents, axis=0), values)
        result = (summed[:, :LANES] / summed[:, LANES:]).astype(jnp.bfloat16).astype(jnp.float32)
        return [result[j * rows:(j + 1) * rows] for j in range(len(blocks))]

    rim_block = jnp.concatenate(
        [q_rim[:, h * LANES:(h + 1) * LANES] for h in range(n)], axis=0)
    rim_pos = base - RIM + lax.rem(row_iota, RIM)
    rim_bias = bias_of(rim_pos)
    bias = bias_of(own_pos)

    def recv_bc(s):
        to_ctx(bc_all.at[s, core], bc_all.at[s, core], bc_send.at[0], bc_recv.at[s], pair).wait_recv()

    crossed = [pair] + [lax.rem(pair + 2 * k, n) for k in range(1, n // 2)]
    for part in range(2):
        order = range(part * n // 2, (part + 1) * n // 2)
        heads = [lax.rem(me + 1 + k, n) for k in order]
        spans = [pl.ds(pl.multiple_of(h * LANES, LANES), LANES) for h in heads]
        blocks = [q_ref[:, cols] for cols in spans]
        if part == 0:
            results = attention(blocks + [rim_block], [bias] * len(blocks) + [rim_bias])
            gated_ref[0] = results.pop()
        else:
            results = attention(blocks, [bias] * len(blocks))
        outs = []
        for h, cols, attended in zip(heads, spans, results):
            rim = gated_ref[0, pl.ds(pl.multiple_of(h * RIM + RIM - 8, 8), 8), :]
            outs.append(conv(jnp.concatenate([rim, attended], axis=0), taps_ref[:, cols]))
        for k, h, x in zip(order, heads, outs):
            if k < n - 1:
                x_out[h] = x
                to_ctx(x_out.at[h], x_all.at[me], x_send.at[k], x_recv.at[me], h).start()
            else:
                x_all[me] = x
        if part == 0:
            for k, s in enumerate(column):
                recv_bc(s)
                relay_bc(s, n // 2 + k).start()
                share_bc(s, k).start()
        else:
            for k, s in enumerate(crossed):
                recv_bc(s)
                share_bc(s, n // 2 - 1 + k).start()

    upper = (row_iota <= lane_iota).astype(jnp.float32)
    left = lane_iota < LANES // 2
    rate = [rate_ref[2 * me + a] for a in range(2)]
    skip = jnp.where(left[:1], skip_ref[2 * me], skip_ref[2 * me + 1])
    for k in range(1, n):
        s = lax.rem(me + k, n)
        to_ctx(dt_own.at[s], dt_all.at[s], dt_send.at[k], dt_recv.at[s], s).wait_recv()
    dt_rows = [jnp.concatenate([dt_all[i, a:a + 1] for i in range(n)], axis=0) for a in range(2)]
    cum_rows = [jnp.dot(-rate[a] * dt_rows[a], upper, precision=lax.Precision.HIGHEST,
                        preferred_element_type=jnp.float32) for a in range(2)]
    keeps = []
    other = 1 - core
    for k in range(1, n):
        s = lax.rem(me + k, n)
        to_core(bc_all.at[s, other], bc_all.at[s, other], bc_core_send.at[0],
                bc_core_recv.at[s]).wait_recv()
    for i in range(n):
        start = i * rows
        pos = start + row_iota
        first = first_of(pos)
        key_pos = start + lane_iota
        visible = (key_pos >= first) & (key_pos <= pos)
        cum = [cum_rows[a][i:i + 1] for a in range(2)]
        dts = [dt_rows[a][i:i + 1] for a in range(2)]
        side = (rows // 2, LANES)
        cum_col = jnp.concatenate([jnp.broadcast_to(r, side) for r in cum], axis=0).T
        dt_col = jnp.concatenate([jnp.broadcast_to(r, side) for r in dts], axis=0).T
        gram = jnp.where(visible, dot_nt(bc_all[i, 1], bc_all[i, 0]), 0.0)
        for a in range(2):
            col = cum_col[:, a * (LANES // 2):a * (LANES // 2) + 1]
            gap = jnp.where(visible, col - cum[a], 0.0)
            mix_ref[i, :, a * LANES:(a + 1) * LANES] = (
                gram * jnp.exp(gap) * dts[a]).astype(jnp.bfloat16)
        last_start = first[rows - 1:rows]
        cum_last = cum_col[rows - 1:rows]
        carry_ref[i] = jnp.where(first < start, jnp.exp(cum_col), 0.0)
        weight_ref[i] = jnp.where(pos >= last_start, jnp.exp(cum_last - cum_col) * dt_col, 0.0)
        keeps.append(jnp.where(last_start < start, jnp.exp(cum_last), 0.0))

    state = jnp.zeros((state_size, LANES), jnp.float32)
    for k in range(1, n):
        s = lax.rem(me + n - k, n)
        to_ctx(x_all.at[s], x_all.at[s], x_send.at[0], x_recv.at[s], pair).wait_recv()
    for i in range(n):
        state_ref[i] = state.astype(jnp.bfloat16)
        if i < n - 1:
            weighted = (x_all[i].astype(jnp.float32) * weight_ref[i]).astype(jnp.bfloat16)
            state = keeps[i] * state + dot_tn(bc_all[i, 0], weighted)

    for k in range(n):
        i = lax.rem(me + 1 + k, n)
        xw = x_all[i].astype(jnp.float32)
        both = jnp.concatenate([jnp.where(left, xw, 0.0), jnp.where(left, 0.0, xw)], axis=0)
        y = dot_nn(mix_ref[i], both.astype(jnp.bfloat16)) + skip * xw
        y = (y + carry_ref[i] * dot_nn(bc_all[i, 1], state_ref[i])).astype(jnp.bfloat16)
        if k < n - 1:
            y_out[i] = y
            to_ctx(y_out.at[i], y_all.at[me], y_send.at[i], y_recv.at[me], i).start()
        else:
            y_all[me] = y

    squares = jnp.zeros((rows, LANES), jnp.float32)
    for k in range(n):
        h = lax.rem(me + n - 1 - k, n)
        if k < n - 1:
            to_ctx(y_out.at[h], y_all.at[h], y_send.at[h], y_recv.at[h], h).wait_recv()
        z = gate_ref[:, pl.ds(pl.multiple_of(h * LANES, LANES), LANES)].astype(jnp.float32)
        gated = y_all[h].astype(jnp.float32) * silu(z)
        gated_ref[h] = gated
        squares = squares + gated * gated
    sq_own[...] = squares
    swap = to_core(sq_own, sq_other, sq_sem.at[0], sq_sem.at[1])
    swap.start()

    for wanted, copy in direct:
        @pl.when(wanted)
        def _():
            copy.wait_send()
    for j, r in enumerate(range(0, window, 2)):
        @pl.when(even & (me >= r))
        def _():
            relay_even[j].wait_send()
    for j, r in enumerate(range(2, window + 1, 2)):
        @pl.when(odd & (me >= r))
        def _():
            relay_odd[j].wait_send()

    @pl.when(me + 1 < n)
    def _():
        rim_q.wait_send()
        rim_b.wait_send()
    for copy in bc_own:
        copy.wait_send()
    for k, s in enumerate(column):
        relay_bc(s, n // 2 + k).wait_send()
        share_bc(s, k).wait_send()
    for k, s in enumerate(crossed):
        share_bc(s, n // 2 - 1 + k).wait_send()
    for k in range(n - 1):
        h = lax.rem(me + 1 + k, n)
        to_ctx(x_out.at[h], x_all.at[me], x_send.at[k], x_recv.at[me], h).wait_send()
        to_ctx(dt_own.at[h], dt_all.at[me], dt_send.at[k + 1], dt_recv.at[me], h).wait_send()
    for i in range(n):
        @pl.when(me != i)
        def _():
            to_ctx(y_out.at[i], y_all.at[me], y_send.at[i], y_recv.at[me], i).wait_send()
    swap.wait()
    width = 2 * n * LANES
    mean_square = jnp.sum(sq_own[...] + sq_other[...], axis=1, keepdims=True) / width
    factor = lax.rsqrt(mean_square + EPSILON)
    for h in range(n):
        cols = slice(h * LANES, (h + 1) * LANES)
        out_ref[:, cols] = (gated_ref[h] * factor * gain_ref[:, cols]).astype(jnp.bfloat16)


def fused_on_device(
    queries, key_rows, value_rows, doc_lengths, gate_input, bc_input, step_size,
    decay_rate, skip_gain, conv_x, conv_bc, norm_gain,
):
    n = lax.axis_size("ctx")
    rows = queries.shape[0]
    state_size = bc_input.shape[3]
    longest = n * rows // 2 + 64
    window = 1 + -(-(longest - 1) // rows)
    bc = bc_input.reshape(rows, -1)
    bf16, f32 = jnp.bfloat16, jnp.float32
    vmem = pl.BlockSpec(memory_space=pltpu.VMEM)
    smem = pl.BlockSpec(memory_space=pltpu.SMEM)
    dma = pltpu.SemaphoreType.DMA
    half = window // 2
    return pl.pallas_call(
        functools.partial(fused_kernel, n, window),
        out_shape=jax.ShapeDtypeStruct(queries.shape, bf16),
        in_specs=[smem] * 3 + [pl.BlockSpec(memory_space=pl.ANY)] * 9,
        out_specs=vmem,
        scratch_shapes=[
            pltpu.VMEM(queries.shape, bf16),
            pltpu.VMEM(gate_input.shape, bf16),
            pltpu.VMEM(bc.shape, bf16),
            pltpu.VMEM(step_size.shape[::-1], f32),
            pltpu.VMEM(conv_x.shape, f32),
            pltpu.VMEM(conv_bc.shape, f32),
            pltpu.VMEM((1, norm_gain.shape[0]), f32),
            dma((9,)),
            pltpu.VMEM((window + 1, 2, rows, LANES), bf16),
            pltpu.VMEM((RIM, queries.shape[1]), bf16),
            pltpu.VMEM((RIM, bc.shape[1]), bf16),
            pltpu.VMEM((n, 2, rows, state_size), bf16),
            pltpu.VMEM((n, rows, LANES), bf16),
            pltpu.VMEM((n, rows, LANES), bf16),
            pltpu.VMEM((n, 8, LANES), f32),
            pltpu.VMEM((n, 8, LANES), f32),
            pltpu.VMEM((n, rows, 2 * LANES), bf16),
            pltpu.VMEM((n, rows, LANES), f32),
            pltpu.VMEM((n, rows, LANES), f32),
            pltpu.VMEM((n, state_size, LANES), bf16),
            pltpu.VMEM((n, rows, LANES), bf16),
            pltpu.VMEM((n, rows, LANES), bf16),
            pltpu.VMEM((n, rows, LANES), f32),
            pltpu.VMEM((rows, LANES), f32),
            pltpu.VMEM((rows, LANES), f32),
            dma((half + 2 + window,)),
            dma((window + 1,)),
            dma((2,)),
            dma((2,)),
            dma((n,)),
            dma((n,)),
            dma((n,)),
            dma((n,)),
            dma((n,)),
            dma((n,)),
            dma((n,)),
            dma((n,)),
            dma((n,)),
            dma((n,)),
            dma((2,)),
        ],
        compiler_params=pltpu.CompilerParams(
            collective_id=0, has_side_effects=True, vmem_limit_bytes=58 * 1024 * 1024),
    )(
        doc_lengths, decay_rate, skip_gain, queries, key_rows, value_rows, gate_input, bc, step_size.T,
        conv_x, conv_bc, norm_gain.reshape(1, -1),
    )


def plan(queries, key_rows, *rest):
    blocks = queries.shape[1] // LANES
    if blocks == lax.axis_size("ctx") and queries.shape[0] == LANES:
        return fused_on_device(queries, key_rows, *rest)
    return on_device(queries, key_rows, *rest)


def solution(mesh):
    return jax.shard_map(
        plan,
        mesh=mesh,
        in_specs=(
            P("ctx", "tp"),
            P("ctx", "tp"),
            P("ctx", "tp"),
            P(),
            P("ctx", "tp"),
            P("ctx", None, None, None),
            P("ctx", "tp"),
            P("tp"),
            P("tp"),
            P(None, "tp"),
            P(),
            P("tp"),
        ),
        out_specs=P("ctx", "tp"),
        check_vma=False,
    )
```

```python
import functools
import math

import jax
import jax.numpy as jnp
from jax import lax
from jax.experimental import pallas as pl
from jax.experimental.pallas import tpu as pltpu
from jax.sharding import PartitionSpec as P

EPSILON = 1e-05
NEGATIVE_FILL = -1e30


def from_behind(x, axis, by):
    size = lax.axis_size(axis)
    pairs = [(i, i + by) for i in range(size) if 0 <= i + by < size]
    return lax.ppermute(x, axis, pairs)


def prefix(x, axis, combine, identity):
    size, mine = (lax.axis_size(axis), lax.axis_index(axis))
    everything = jax.tree.map(
        lambda part, kind: lax.all_gather(part.astype(kind), axis), x, (jnp.bfloat16, jnp.bfloat16)
    )
    start = jax.tree.map(
        lambda part, zero: jnp.broadcast_to(jnp.asarray(zero, part.dtype), part.shape), x, identity
    )

    def step(k, before):
        reached = k < mine
        new = combine(
            before, jax.tree.map(lambda part, own: part[k].astype(own.dtype), everything, x)
        )
        return jax.tree.map(lambda a, b: jnp.where(reached, a, b), new, before)

    return lax.fori_loop(0, size, step, start)


def swapped(block, axis, bit):
    count = lax.axis_size(axis)
    route = []
    for low in range(count):
        high = low | 1 << bit
        if high != low and high < count:
            route += [(low, high), (high, low)]
    return lax.ppermute(block, axis, route)


def first_positions(doc_lengths, positions):
    doc_ends = jnp.cumsum(doc_lengths)
    doc_starts = doc_ends - doc_lengths
    covered = doc_starts[None, :] <= positions[:, None]
    return jnp.max(
        jnp.where(covered, doc_starts[None, :], jnp.zeros_like(doc_starts)[None, :]), axis=1
    )


def attend(
    running, key_block, value_block, key_start, query_rows, query_pos, query_first, score_scale
):
    maximum, totals, summed = running
    key_pos = key_start + jnp.arange(key_block.shape[0], dtype=jnp.int32)
    scores = (
        jnp.einsum("qhd,kd->hqk", query_rows, key_block, preferred_element_type=jnp.float32)
        * score_scale
    )
    visible = (
        (key_pos[None, :] <= query_pos[:, None]) & (key_pos[None, :] >= query_first[:, None])
    )[None]
    masked = jnp.where(visible, scores, NEGATIVE_FILL)
    new_maximum = jnp.maximum(maximum, jnp.max(masked, axis=-1))
    exponent = jnp.where(visible, jnp.exp(masked - new_maximum[..., None]), 0.0)
    factor = jnp.exp(maximum - new_maximum)
    totals = totals * factor + jnp.sum(exponent, axis=-1)
    weights = exponent.astype(jnp.bfloat16)
    summed = summed * factor[..., None] + jnp.einsum(
        "hqk,kd->hqd", weights, value_block, preferred_element_type=jnp.float32
    )
    return (new_maximum, totals, summed)


def key_folder(query_rows, query_pos, query_first, score_scale):
    query_last = jnp.max(query_pos)
    earliest = jnp.min(query_first)

    def maybe_attend(running, key_slab, value_slab, key_start):
        needed = (key_start <= query_last) & (key_start + key_slab.shape[0] > earliest)

        def compute(inner_run):
            return attend(
                inner_run,
                key_slab,
                value_slab,
                key_start,
                query_rows,
                query_pos,
                query_first,
                score_scale,
            )

        def keep(inner_run):
            return inner_run

        return lax.cond(needed, compute, keep, running)

    def fold_keys(running, pieces, offset):
        key_block, value_block = pieces
        key_count = key_block.shape[0]
        block_width = 256
        block_count = key_count // block_width

        def visit(inner_run, entries):
            block_index, key_slab, value_slab = entries
            return (maybe_attend(inner_run, key_slab, value_slab, block_index * block_width), None)

        running, _ = lax.scan(
            visit,
            running,
            (
                jnp.arange(block_count, dtype=jnp.int32),
                key_block.reshape(block_count, block_width, -1),
                value_block.reshape(block_count, block_width, -1),
            ),
        )
        return running

    return fold_keys


def finish(running, row_count):
    maximum, totals, summed = running
    output = summed / totals[..., None]
    return jnp.transpose(output, (1, 0, 2)).reshape(row_count, -1).astype(jnp.bfloat16)


def causal_local(extended, taps, positions, first_token, tap_count):
    row_count = positions.shape[0]
    accumulated = jnp.zeros((row_count,) + extended.shape[1:], jnp.float32)
    for shift_by in range(tap_count):
        tap_rows = extended[tap_count - 1 - shift_by : tap_count - 1 - shift_by + row_count].astype(
            jnp.float32
        )
        usable = (positions - shift_by >= first_token).reshape(
            (row_count,) + (1,) * (extended.ndim - 1)
        )
        accumulated = accumulated + jnp.where(
            usable, tap_rows * taps[tap_count - 1 - shift_by], 0.0
        )
    return accumulated


def combine_states(earlier, following):
    return (earlier[0] * following[0], earlier[1] * following[0][:, None, None] + following[1])


def on_device(
    queries,
    key_rows,
    value_rows,
    doc_lengths,
    gate_input,
    bc_input,
    step_size,
    decay_rate,
    skip_gain,
    conv_x,
    conv_bc,
    norm_gain,
):
    row_count = queries.shape[0]
    head_size = key_rows.shape[1]
    head_count = queries.shape[1] // head_size
    score_scale = 1.0 / math.sqrt(head_size)
    ctx_index = lax.axis_index("ctx")
    block_start = ctx_index * row_count
    own_pos = block_start + jnp.arange(row_count, dtype=jnp.int32)
    own_first = first_positions(doc_lengths, own_pos)
    initial = (
        jnp.full((head_count, row_count), NEGATIVE_FILL, jnp.float32),
        jnp.zeros((head_count, row_count), jnp.float32),
        jnp.zeros((head_count, row_count, head_size), jnp.float32),
    )
    query_rows = queries.reshape(row_count, head_count, head_size)
    running = key_folder(query_rows, own_pos, own_first, score_scale)(
        initial,
        (
            lax.all_gather(key_rows, "ctx", axis=0, tiled=True),
            lax.all_gather(value_rows, "ctx", axis=0, tiled=True),
        ),
        jnp.int32(0),
    )
    attended = finish(running, row_count)
    group_index = lax.axis_index("tp") // 2
    bc_local = lax.dynamic_index_in_dim(bc_input, group_index, 2, keepdims=False)
    conv_bc_local = lax.dynamic_index_in_dim(conv_bc, group_index, 2, keepdims=False)
    tap_count = conv_x.shape[0]
    rim_input, rim_bc = from_behind(
        (attended[row_count - tap_count + 1 :], bc_local[row_count - tap_count + 1 :]), "ctx", 1
    )
    mixed_input = jax.nn.silu(
        causal_local(
            jnp.concatenate([rim_input, attended], 0), conv_x, own_pos, own_first, tap_count
        )
    ).astype(jnp.bfloat16)
    bc_conv = jax.nn.silu(
        causal_local(
            jnp.concatenate([rim_bc, bc_local], 0), conv_bc_local, own_pos, own_first, tap_count
        )
    ).astype(jnp.bfloat16)
    heads_local = step_size.shape[1]
    input_heads = mixed_input.reshape(row_count, heads_local, -1)
    b_values = bc_conv[:, 0]
    c_values = bc_conv[:, 1]
    highest = lax.Precision.HIGHEST
    log_decay = -decay_rate[None, :] * step_size
    cumulated = jnp.cumsum(log_decay, axis=0)
    gram_matrix = jnp.dot(c_values, b_values.T, preferred_element_type=jnp.float32)
    visible = (own_pos[None, :] >= own_first[:, None]) & (own_pos[None, :] <= own_pos[:, None])
    cum_heads = cumulated.T
    log_gap = jnp.where(visible[None], cum_heads[:, :, None] - cum_heads[:, None, :], -jnp.inf)
    mixing = gram_matrix[None] * jnp.exp(log_gap) * step_size.T[:, None, :]
    input_wide = input_heads.astype(jnp.float32)
    inner_part = jnp.einsum("hts,shp->thp", mixing, input_wide, precision=highest)
    last_start = own_first[-1]
    state_weight = jnp.where(
        (own_pos >= last_start)[:, None], jnp.exp(cumulated[-1][None, :] - cumulated), 0.0
    )
    state_weight = state_weight * step_size
    block_state = jnp.einsum(
        "shp,sn->hpn",
        state_weight[:, :, None] * input_wide,
        b_values.astype(jnp.float32),
        precision=highest,
    )
    carry_decay = jnp.where(last_start < block_start, jnp.exp(cumulated[-1]), 0.0)
    identity = (jnp.ones_like(carry_decay), jnp.zeros_like(block_state))
    _, incoming = prefix((carry_decay, block_state), "ctx", combine_states, identity)
    carry_in = (own_first < block_start).astype(jnp.float32)
    carried_part = jnp.einsum(
        "tn,hpn->thp", c_values.astype(jnp.float32), incoming, precision=highest
    )
    carried_part = carried_part * (jnp.exp(cumulated) * carry_in[:, None])[:, :, None]
    ssm_out = inner_part + carried_part + skip_gain[None, :, None] * input_wide
    gated = ssm_out.reshape(row_count, -1) * jax.nn.silu(gate_input.astype(jnp.float32))
    square_sum = jnp.sum(gated * gated, axis=1)
    partner_sum = swapped(square_sum, "tp", 0)
    mean_square = (square_sum + partner_sum) / (2 * gated.shape[1])
    return (gated * lax.rsqrt(mean_square + EPSILON)[:, None] * norm_gain[None, :]).astype(
        jnp.bfloat16
    )


LANES = 128
RIM = 16
MESH = pl.DeviceIdType.MESH


def dot_nt(a, b):
    return lax.dot_general(a, b, (((1,), (1,)), ((), ())), preferred_element_type=jnp.float32)


def dot_tn(a, b):
    return lax.dot_general(a, b, (((0,), (0,)), ((), ())), preferred_element_type=jnp.float32)


def dot_nn(a, b):
    return jnp.dot(a, b, preferred_element_type=jnp.float32)


def silu(v):
    return v / (1.0 + jnp.exp(-v))


def fused_kernel(
    n,
    window,
    doc_ref,
    rate_ref,
    skip_ref,
    q_in,
    k_in,
    v_in,
    gate_in,
    bc_in,
    step_in,
    taps_in,
    bc_taps_in,
    gain_in,
    out_ref,
    q_ref,
    gate_ref,
    bc_ref,
    step_ref,
    taps_ref,
    bc_taps_ref,
    gain_ref,
    load_sem,
    kv,
    q_rim,
    bc_rim,
    bc_all,
    x_out,
    x_all,
    dt_own,
    dt_all,
    mix_ref,
    weight_ref,
    carry_ref,
    state_ref,
    y_out,
    y_all,
    gated_ref,
    sq_own,
    sq_other,
    kv_send,
    kv_recv,
    rim_send,
    rim_recv,
    bc_send,
    bc_recv,
    bc_core_send,
    bc_core_recv,
    x_send,
    x_recv,
    dt_send,
    dt_recv,
    y_send,
    y_recv,
    sq_sem,
):
    loads = [
        pltpu.make_async_copy(src, dst, load_sem.at[i])
        for i, (src, dst) in enumerate((
            (k_in, kv.at[0, 0]), (v_in, kv.at[0, 1]), (bc_in, bc_ref), (q_in, q_ref),
            (step_in, step_ref), (bc_taps_in, bc_taps_ref), (taps_in, taps_ref),
            (gate_in, gate_ref), (gain_in, gain_ref)))
    ]
    for load in loads:
        load.start()
    rows = q_ref.shape[0]
    me = lax.axis_index("ctx")
    tp = lax.axis_index("tp")
    core = lax.rem(tp, 2)
    group = tp // 2
    tp_other = tp + 1 - 2 * core
    parity = lax.rem(me, 2)
    pair = me + 1 - 2 * parity
    state_size = bc_all.shape[3]
    ndoc = doc_ref.shape[0]
    groups = bc_ref.shape[1] // (2 * state_size)

    def to_ctx(src, dst, send, recv, where):
        return pltpu.make_async_remote_copy(
            src_ref=src, dst_ref=dst, send_sem=send, recv_sem=recv,
            device_id=(where, tp), device_id_type=MESH)

    def to_core(src, dst, send, recv):
        return pltpu.make_async_remote_copy(
            src_ref=src, dst_ref=dst, send_sem=send, recv_sem=recv,
            device_id=(me, tp_other), device_id_type=MESH)

    barrier = pltpu.get_barrier_semaphore()
    for k in range(1, n):
        pl.semaphore_signal(
            barrier, inc=1, device_id=(lax.rem(me + k, n), tp), device_id_type=MESH)
    pl.semaphore_signal(barrier, inc=1, device_id=(me, tp_other), device_id_type=MESH)
    for r in range(1, window):
        @pl.when(me < r)
        def _():
            kv[r] = jnp.zeros(kv.shape[1:], kv.dtype)

    @pl.when(me == 0)
    def _():
        q_rim[...] = jnp.zeros(q_rim.shape, q_rim.dtype)
        bc_rim[...] = jnp.zeros(bc_rim.shape, bc_rim.dtype)

    for load in loads:
        load.wait()
    steps = step_ref[...]
    for d in range(n):
        dt_own[d, 0:2] = steps[2 * d:2 * d + 2]

    pl.semaphore_wait(barrier, n)

    half = window // 2
    direct = []
    for k in range(1, half + 1):
        copy = to_ctx(kv.at[0], kv.at[2 * k], kv_send.at[k], kv_recv.at[2 * k],
                      jnp.minimum(me + 2 * k, n - 1))
        wanted = me + 2 * k < n
        if 2 * k >= window:
            wanted = wanted & (parity == 1)
        direct.append((wanted, copy))
    even = parity == 0
    odd = parity == 1
    relay_even = [to_ctx(kv.at[r], kv.at[r + 1], kv_send.at[half + 1 + r], kv_recv.at[r + 1], pair)
                  for r in range(0, window, 2)]
    relay_odd = [to_ctx(kv.at[r], kv.at[r - 1], kv_send.at[half + 1 + r], kv_recv.at[r - 1], pair)
                 for r in range(2, window + 1, 2)]
    nxt = jnp.minimum(me + 1, n - 1)
    rim_q = to_ctx(q_ref.at[pl.ds(rows - RIM, RIM)], q_rim, rim_send.at[0], rim_recv.at[0], nxt)
    rim_b = to_ctx(bc_ref.at[pl.ds(rows - RIM, RIM)], bc_rim, rim_send.at[1], rim_recv.at[1], nxt)

    @pl.when(me + 1 < n)
    def _():
        rim_b.start()

    @pl.when(even)
    def _():
        relay_even[0].start()

    for wanted, copy in direct:
        @pl.when(wanted)
        def _():
            copy.start()

    @pl.when(me + 1 < n)
    def _():
        rim_q.start()

    for k in range(1, n):
        d = lax.rem(me + k, n)
        to_ctx(dt_own.at[d], dt_all.at[me], dt_send.at[k], dt_recv.at[me], d).start()
    dt_all[me] = dt_own[me]

    starts = []
    total = jnp.int32(0)
    for i in range(ndoc):
        starts.append(total)
        total = total + doc_ref[i]

    def first_of(pos):
        first = jnp.zeros_like(pos)
        for s in starts:
            first = jnp.where(s <= pos, s, first)
        return first

    row_iota = lax.broadcasted_iota(jnp.int32, (rows, LANES), 0)
    lane_iota = lax.broadcasted_iota(jnp.int32, (rows, LANES), 1)
    base = me * rows
    own_pos = base + row_iota
    own_first = first_of(own_pos)
    tap_count = taps_ref.shape[0]
    since = own_pos - own_first

    def conv(extended, taps):
        acc = None
        for m in range(tap_count):
            part = extended[8 - m: 8 - m + rows] * taps[tap_count - 1 - m: tap_count - m]
            part = jnp.where(since >= m, part, 0.0)
            acc = part if acc is None else acc + part
        return silu(acc).astype(jnp.bfloat16)

    @pl.when(me > 0)
    def _():
        rim_b.wait_recv()

    for i in range(2):
        for piece in range(state_size // LANES):
            cols = pl.ds(pl.multiple_of(
                (i * groups + group) * state_size + piece * LANES, LANES), LANES)
            extended = jnp.concatenate(
                [bc_rim[:, cols].astype(jnp.float32)[RIM - 8:], bc_ref[:, cols].astype(jnp.float32)], axis=0)
            lanes = slice(piece * LANES, (piece + 1) * LANES)
            taps = jnp.zeros((tap_count, LANES), jnp.float32)
            for g in range(groups):
                part = jnp.concatenate(
                    [bc_taps_ref[m, i, g:g + 1, lanes] for m in range(tap_count)], axis=0)
                taps = jnp.where(group == g, part, taps)
            bc_all[me, i, :, piece * LANES:(piece + 1) * LANES] = conv(extended, taps)

    column = [lax.rem(me + 2 * k, n) for k in range(1, n // 2)]

    def relay_bc(s, slot):
        return to_ctx(bc_all.at[s, core], bc_all.at[s, core], bc_send.at[slot], bc_recv.at[s], pair)

    def share_bc(s, slot):
        return to_core(bc_all.at[s, core], bc_all.at[s, core], bc_core_send.at[slot], bc_core_recv.at[s])

    bc_own = [to_ctx(bc_all.at[me, core], bc_all.at[me, core], bc_send.at[0], bc_recv.at[me], pair)]
    for k, d in enumerate(column):
        bc_own.append(to_ctx(bc_all.at[me, core], bc_all.at[me, core],
                             bc_send.at[1 + k], bc_recv.at[me], d))

    def bias_of(pos):
        first = first_of(pos)
        parts = []
        for r in range(window):
            key_pos = (me - r) * rows + lane_iota
            parts.append(jnp.where((key_pos <= pos) & (key_pos >= first), 0.0, NEGATIVE_FILL))
        return jnp.concatenate(parts, axis=1)

    rim_pos = base - RIM + lax.rem(row_iota, RIM)
    rim_bias = bias_of(rim_pos)
    bias = bias_of(own_pos)

    for r in range(2, window + 1, 2):
        cond = me >= r
        if r >= window:
            cond = cond & odd

        @pl.when(cond)
        def _():
            to_ctx(kv.at[0], kv.at[r], kv_send.at[0], kv_recv.at[r], pair).wait_recv()

        if r == 2:
            for copy in bc_own:
                copy.start()
        if r < window:
            @pl.when(even & (me >= r))
            def _():
                relay_even[r // 2].start()

        @pl.when(odd & (me >= r))
        def _():
            relay_odd[r // 2 - 1].start()
    for r in range(1, window, 2):
        @pl.when(me >= r)
        def _():
            to_ctx(kv.at[0], kv.at[r], kv_send.at[0], kv_recv.at[r], pair).wait_recv()

    @pl.when(me > 0)
    def _():
        rim_q.wait_recv()

    keys = jnp.concatenate([kv[r, 0] for r in range(window)], axis=0)
    values = jnp.concatenate([kv[r, 1] for r in range(window)], axis=0)
    values = jnp.concatenate([values, jnp.ones_like(values)], axis=1)
    scale = math.log2(math.e) / math.sqrt(k_in.shape[1])

    def attention(blocks, biases):
        scores = dot_nt(jnp.concatenate(blocks, axis=0), keys)
        exponents = []
        for j, bias in enumerate(biases):
            part = scores[j * rows:(j + 1) * rows] + bias
            exponents.append(jnp.exp2(
                (part - jnp.max(part, axis=1, keepdims=True)) * scale).astype(jnp.bfloat16))
        summed = dot_nn(jnp.concatenate(exponents, axis=0), values)
        result = (summed[:, :LANES] / summed[:, LANES:]).astype(jnp.bfloat16).astype(jnp.float32)
        return [result[j * rows:(j + 1) * rows] for j in range(len(blocks))]

    rim_block = jnp.concatenate(
        [q_rim[:, h * LANES:(h + 1) * LANES] for h in range(n)], axis=0)

    def recv_bc(s):
        to_ctx(bc_all.at[s, core], bc_all.at[s, core], bc_send.at[0], bc_recv.at[s], pair).wait_recv()

    crossed = [pair] + [lax.rem(pair + 2 * k, n) for k in range(1, n // 2)]
    for part in range(2):
        order = range(part * n // 2, (part + 1) * n // 2)
        heads = [lax.rem(me + 1 + k, n) for k in order]
        spans = [pl.ds(pl.multiple_of(h * LANES, LANES), LANES) for h in heads]
        blocks = [q_ref[:, cols] for cols in spans]
        if part == 0:
            results = attention(blocks + [rim_block], [bias] * len(blocks) + [rim_bias])
            gated_ref[0] = results.pop()
        else:
            results = attention(blocks, [bias] * len(blocks))
        outs = []
        for h, cols, attended in zip(heads, spans, results):
            rim = gated_ref[0, pl.ds(pl.multiple_of(h * RIM + RIM - 8, 8), 8), :]
            outs.append(conv(jnp.concatenate([rim, attended], axis=0), taps_ref[:, cols]))
        for k, h, x in zip(order, heads, outs):
            if k < n - 1:
                x_out[h] = x
                to_ctx(x_out.at[h], x_all.at[me], x_send.at[k], x_recv.at[me], h).start()
            else:
                x_all[me] = x
        if part == 0:
            for k, s in enumerate(column):
                recv_bc(s)
                relay_bc(s, n // 2 + k).start()
                share_bc(s, k).start()
        else:
            for k, s in enumerate(crossed):
                recv_bc(s)
                share_bc(s, n // 2 - 1 + k).start()

    upper = (row_iota <= lane_iota).astype(jnp.float32)
    left = lane_iota < LANES // 2
    rate = [rate_ref[2 * me + a] for a in range(2)]
    skip = jnp.where(left[:1], skip_ref[2 * me], skip_ref[2 * me + 1])
    for k in range(1, n):
        s = lax.rem(me + k, n)
        to_ctx(dt_own.at[s], dt_all.at[s], dt_send.at[k], dt_recv.at[s], s).wait_recv()
    dt_rows = [jnp.concatenate([dt_all[i, a:a + 1] for i in range(n)], axis=0) for a in range(2)]
    cum_rows = [jnp.dot(-rate[a] * dt_rows[a], upper, precision=lax.Precision.HIGHEST,
                        preferred_element_type=jnp.float32) for a in range(2)]
    keeps = []
    other = 1 - core
    for k in range(1, n):
        s = lax.rem(me + k, n)
        to_core(bc_all.at[s, other], bc_all.at[s, other], bc_core_send.at[0],
                bc_core_recv.at[s]).wait_recv()
    for i in range(n):
        start = i * rows
        pos = start + row_iota
        first = first_of(pos)
        key_pos = start + lane_iota
        visible = (key_pos >= first) & (key_pos <= pos)
        cum = [cum_rows[a][i:i + 1] for a in range(2)]
        dts = [dt_rows[a][i:i + 1] for a in range(2)]
        side = (rows // 2, LANES)
        cum_col = jnp.concatenate([jnp.broadcast_to(r, side) for r in cum], axis=0).T
        dt_col = jnp.concatenate([jnp.broadcast_to(r, side) for r in dts], axis=0).T
        gram = jnp.where(visible, dot_nt(bc_all[i, 1], bc_all[i, 0]), 0.0)
        for a in range(2):
            col = cum_col[:, a * (LANES // 2):a * (LANES // 2) + 1]
            gap = jnp.where(visible, col - cum[a], 0.0)
            mix_ref[i, :, a * LANES:(a + 1) * LANES] = (
                gram * jnp.exp(gap) * dts[a]).astype(jnp.bfloat16)
        last_start = first[rows - 1:rows]
        cum_last = cum_col[rows - 1:rows]
        carry_ref[i] = jnp.where(first < start, jnp.exp(cum_col), 0.0)
        weight_ref[i] = jnp.where(pos >= last_start, jnp.exp(cum_last - cum_col) * dt_col, 0.0)
        keeps.append(jnp.where(last_start < start, jnp.exp(cum_last), 0.0))

    state = jnp.zeros((state_size, LANES), jnp.float32)
    for k in range(1, n):
        s = lax.rem(me + n - k, n)
        to_ctx(x_all.at[s], x_all.at[s], x_send.at[0], x_recv.at[s], pair).wait_recv()
    for i in range(n):
        state_ref[i] = state.astype(jnp.bfloat16)
        if i < n - 1:
            weighted = (x_all[i].astype(jnp.float32) * weight_ref[i]).astype(jnp.bfloat16)
            state = keeps[i] * state + dot_tn(bc_all[i, 0], weighted)

    for k in range(n):
        i = lax.rem(me + 1 + k, n)
        xw = x_all[i].astype(jnp.float32)
        both = jnp.concatenate([jnp.where(left, xw, 0.0), jnp.where(left, 0.0, xw)], axis=0)
        y = dot_nn(mix_ref[i], both.astype(jnp.bfloat16)) + skip * xw
        y = (y + carry_ref[i] * dot_nn(bc_all[i, 1], state_ref[i])).astype(jnp.bfloat16)
        if k < n - 1:
            y_out[i] = y
            to_ctx(y_out.at[i], y_all.at[me], y_send.at[i], y_recv.at[me], i).start()
        else:
            y_all[me] = y

    squares = jnp.zeros((rows, LANES), jnp.float32)
    for k in range(n):
        h = lax.rem(me + n - 1 - k, n)
        if k < n - 1:
            to_ctx(y_out.at[h], y_all.at[h], y_send.at[h], y_recv.at[h], h).wait_recv()
        z = gate_ref[:, pl.ds(pl.multiple_of(h * LANES, LANES), LANES)].astype(jnp.float32)
        gated = y_all[h].astype(jnp.float32) * silu(z)
        gated_ref[h] = gated
        squares = squares + gated * gated
    sq_own[...] = squares
    swap = to_core(sq_own, sq_other, sq_sem.at[0], sq_sem.at[1])
    swap.start()

    for wanted, copy in direct:
        @pl.when(wanted)
        def _():
            copy.wait_send()
    for j, r in enumerate(range(0, window, 2)):
        @pl.when(even & (me >= r))
        def _():
            relay_even[j].wait_send()
    for j, r in enumerate(range(2, window + 1, 2)):
        @pl.when(odd & (me >= r))
        def _():
            relay_odd[j].wait_send()

    @pl.when(me + 1 < n)
    def _():
        rim_q.wait_send()
        rim_b.wait_send()
    for copy in bc_own:
        copy.wait_send()
    for k, s in enumerate(column):
        relay_bc(s, n // 2 + k).wait_send()
        share_bc(s, k).wait_send()
    for k, s in enumerate(crossed):
        share_bc(s, n // 2 - 1 + k).wait_send()
    for k in range(n - 1):
        h = lax.rem(me + 1 + k, n)
        to_ctx(x_out.at[h], x_all.at[me], x_send.at[k], x_recv.at[me], h).wait_send()
        to_ctx(dt_own.at[h], dt_all.at[me], dt_send.at[k + 1], dt_recv.at[me], h).wait_send()
    for i in range(n):
        @pl.when(me != i)
        def _():
            to_ctx(y_out.at[i], y_all.at[me], y_send.at[i], y_recv.at[me], i).wait_send()
    swap.wait()
    width = 2 * n * LANES
    mean_square = jnp.sum(sq_own[...] + sq_other[...], axis=1, keepdims=True) / width
    factor = lax.rsqrt(mean_square + EPSILON)
    for h in range(n):
        cols = slice(h * LANES, (h + 1) * LANES)
        out_ref[:, cols] = (gated_ref[h] * factor * gain_ref[:, cols]).astype(jnp.bfloat16)


def fused_on_device(
    queries, key_rows, value_rows, doc_lengths, gate_input, bc_input, step_size,
    decay_rate, skip_gain, conv_x, conv_bc, norm_gain,
):
    n = lax.axis_size("ctx")
    rows = queries.shape[0]
    state_size = bc_input.shape[3]
    longest = n * rows // 2 + 64
    window = 1 + -(-(longest - 1) // rows)
    bc = bc_input.reshape(rows, -1)
    bf16, f32 = jnp.bfloat16, jnp.float32
    vmem = pl.BlockSpec(memory_space=pltpu.VMEM)
    smem = pl.BlockSpec(memory_space=pltpu.SMEM)
    dma = pltpu.SemaphoreType.DMA
    half = window // 2
    return pl.pallas_call(
        functools.partial(fused_kernel, n, window),
        out_shape=jax.ShapeDtypeStruct(queries.shape, bf16),
        in_specs=[smem] * 3 + [pl.BlockSpec(memory_space=pl.ANY)] * 9,
        out_specs=vmem,
        scratch_shapes=[
            pltpu.VMEM(queries.shape, bf16),
            pltpu.VMEM(gate_input.shape, bf16),
            pltpu.VMEM(bc.shape, bf16),
            pltpu.VMEM(step_size.shape[::-1], f32),
            pltpu.VMEM(conv_x.shape, f32),
            pltpu.VMEM(conv_bc.shape, f32),
            pltpu.VMEM((1, norm_gain.shape[0]), f32),
            dma((9,)),
            pltpu.VMEM((window + 1, 2, rows, LANES), bf16),
            pltpu.VMEM((RIM, queries.shape[1]), bf16),
            pltpu.VMEM((RIM, bc.shape[1]), bf16),
            pltpu.VMEM((n, 2, rows, state_size), bf16),
            pltpu.VMEM((n, rows, LANES), bf16),
            pltpu.VMEM((n, rows, LANES), bf16),
            pltpu.VMEM((n, 8, LANES), f32),
            pltpu.VMEM((n, 8, LANES), f32),
            pltpu.VMEM((n, rows, 2 * LANES), bf16),
            pltpu.VMEM((n, rows, LANES), f32),
            pltpu.VMEM((n, rows, LANES), f32),
            pltpu.VMEM((n, state_size, LANES), bf16),
            pltpu.VMEM((n, rows, LANES), bf16),
            pltpu.VMEM((n, rows, LANES), bf16),
            pltpu.VMEM((n, rows, LANES), f32),
            pltpu.VMEM((rows, LANES), f32),
            pltpu.VMEM((rows, LANES), f32),
            dma((half + 2 + window,)),
            dma((window + 1,)),
            dma((2,)),
            dma((2,)),
            dma((n,)),
            dma((n,)),
            dma((n,)),
            dma((n,)),
            dma((n,)),
            dma((n,)),
            dma((n,)),
            dma((n,)),
            dma((n,)),
            dma((n,)),
            dma((2,)),
        ],
        compiler_params=pltpu.CompilerParams(
            collective_id=0, has_side_effects=True, vmem_limit_bytes=58 * 1024 * 1024),
    )(
        doc_lengths, decay_rate, skip_gain, queries, key_rows, value_rows, gate_input, bc, step_size.T,
        conv_x, conv_bc, norm_gain.reshape(1, -1),
    )


def plan(queries, key_rows, *rest):
    blocks = queries.shape[1] // LANES
    if blocks == lax.axis_size("ctx") and queries.shape[0] == LANES:
        return fused_on_device(queries, key_rows, *rest)
    return on_device(queries, key_rows, *rest)


def solution(mesh):
    return jax.shard_map(
        plan,
        mesh=mesh,
        in_specs=(
            P("ctx", "tp"),
            P("ctx", "tp"),
            P("ctx", "tp"),
            P(),
            P("ctx", "tp"),
            P("ctx", None, None, None),
            P("ctx", "tp"),
            P("tp"),
            P("tp"),
            P(None, "tp"),
            P(),
            P("tp"),
        ),
        out_specs=P("ctx", "tp"),
        check_vma=False,
    )
```
